512 devices in a mesh: shot: 16 (over z, core), gx: 8 (over y), gy: 4 (over x).
Axes of the slice: x: 4, y: 8, z: 8, core: 2. Of those that a mesh axis runs over, the one named last changes fastest.
Arguments:
- fields_now: float32 [16, 4, 8, 512, 512], P('shot', None, None, 'gx', 'gy'), may hold values from -6 to 6
- fields_before: float32 [16, 4, 8, 512, 512], P('shot', None, None, 'gx', 'gy'), may hold values from -6 to 6
- speed_sq: float32 [8, 512, 512], P(None, 'gx', 'gy'), may hold values from 0.04 to 0.16
- born_dir: float32 [8, 512, 512], P(None, 'gx', 'gy'), may hold values from -1.5 to 1.5
- pml_x: int32 [512], replicated, may hold values from 0 to 16, as said below
- pml_y: int32 [512], replicated, may hold values from 0 to 16, as said below
- src_x: int32 [16], P('shot'), may hold values from 0 to 511
- src_y: int32 [16], P('shot'), may hold values from 0 to 511
- src_amp: float32 [16, 2], P('shot'), may hold values from -8 to 8
- rec_x: int32 [16, 512], P('shot'), may hold values from 0 to 511
- rec_y: int32 [16, 512], P('shot'), may hold values from 0 to 511
- residual: float32 [16, 2, 512], P('shot'), may hold values from -6 to 6
Outputs:
- fields_after: float32 [16, 4, 8, 512, 512], P('shot', None, None, 'gx', 'gy')
- gradient: float32 [8, 512, 512], P(None, 'gx', 'gy')
- hess_vec: float32 [8, 512, 512], P(None, 'gx', 'gy')
- curvature: float32 [], replicated
The draws below stay inside these ranges and needn't reach their ends.
Inputs may be any that keep to these rules, and one draw needn't show every extreme that they name: pml_x[i] is the larger of max(0, 16 - i) and max(0, w - (511 - i)), with w between 8 and 16 drawn once. pml_y[i] is the larger of max(0, 16 - i) and max(0, w - (511 - i)), with w between 8 and 16 drawn once.
All inputs are finite; a program needn't handle non-finite values.
Results may differ from the reference program's by a relative error of at most 0.00045.
Values sent between devices are 32-bit elements; how exact they have to be, the bound alone decides.
A program may use at most 64 MiB of HBM per device.

```python
import math
import jax
import jax.numpy as jnp
from jax import lax

NZ = 8
NREC = 512
PML_W = 16
NX = 512
NY = 512
SHOTS = 16


def layer_band(key, length):
    far_width = jax.random.randint(key, (), PML_W // 2, PML_W + 1)
    places = jnp.arange(length, dtype=jnp.int32)
    near_side = jnp.maximum(PML_W - places, 0)
    far_side = jnp.maximum(far_width - (length - 1 - places), 0)
    return jnp.maximum(near_side, far_side).astype(jnp.int32)


def draw_pml_x(key, part):
    key = jax.random.fold_in(key, 11)
    return layer_band(key, NX)


def draw_pml_y(key, part):
    key = jax.random.fold_in(key, 23)
    return layer_band(key, NY)


def set_ends(result, own_key, smallest, largest):
    longest = result.shape.index(max(result.shape))
    spots = []
    for shift in (0, 1):
        where = [jax.random.randint(jax.random.fold_in(own_key, axis), (), 0, length) for axis, length in enumerate(result.shape)]
        where[longest] = (where[longest] + shift) % result.shape[longest]
        spots.append(tuple(where))
    return result.at[spots[0]].set(smallest).at[spots[1]].set(largest)


def level_of(key, shape, split, smallest, high):
    gain, own = 1.0, jax.random.fold_in(key, 6)
    for position, parts in split:
        heights = jnp.exp(jax.random.uniform(jax.random.fold_in(own, position), (parts,), jnp.float32, smallest / len(split), high / len(split)))
        gain = gain * jnp.repeat(heights, shape[position] // parts).reshape([-1 if axis == position else 1 for axis in range(len(shape))])
    return gain


def scatter_about(key, dims, scale, limit, shards=(), held_as=jnp.bfloat16):
    array = jax.random.normal(key, dims, jnp.float32) * scale
    if len(shards) > 0:
        array = level_of(key, dims, shards, -0.22, 0.18) * array
    return jnp.clip(array, min=-limit, max=limit).astype(held_as)


def setup_inputs(seed: int = 0) -> dict:
    streams_of = jax.random.split(jax.random.key(seed), 13)
    return {
        "fields_now": scatter_about(streams_of[0], (SHOTS, 4, NZ, NX, NY), 1.0, 6.0, ((0, 16), (3, 8), (4, 4)), jnp.float32),
        "fields_before": scatter_about(streams_of[1], (SHOTS, 4, NZ, NX, NY), 1.0, 6.0, ((0, 16), (3, 8), (4, 4)), jnp.float32),
        "speed_sq": jnp.clip(jnp.exp(math.log(0.16) - 1.3862944 * jax.random.uniform(streams_of[2], (NZ, NX, NY), jnp.float32) ** level_of(streams_of[2], (NZ, NX, NY), ((1, 8), (2, 4)), -0.2, 0.2)), 0.04, 0.16),
        "born_dir": scatter_about(streams_of[3], (NZ, NX, NY), 0.25, 1.5, ((1, 8), (2, 4)), jnp.float32),
        "pml_x": draw_pml_x(jax.random.fold_in(streams_of[12], 71), 0),
        "pml_y": draw_pml_y(jax.random.fold_in(streams_of[12], 71), 0),
        "src_x": set_ends(jax.random.randint(streams_of[6], (SHOTS,), 0, NX), jax.random.fold_in(streams_of[6], 1), 0, NX - 1).astype(jnp.int32),
        "src_y": set_ends(jax.random.randint(streams_of[7], (SHOTS,), 0, NY), jax.random.fold_in(streams_of[7], 1), 0, NY - 1).astype(jnp.int32),
        "src_amp": scatter_about(streams_of[8], (SHOTS, 2), 3.0, 8.0, ((0, 16),), jnp.float32),
        "rec_x": set_ends(jax.random.randint(streams_of[9], (SHOTS, NREC), 0, NX), jax.random.fold_in(streams_of[9], 1), 0, NX - 1).astype(jnp.int32),
        "rec_y": set_ends(jax.random.randint(streams_of[10], (SHOTS, NREC), 0, NY), jax.random.fold_in(streams_of[10], 1), 0, NY - 1).astype(jnp.int32),
        "residual": scatter_about(streams_of[11], (SHOTS, 2, NREC), 1.0, 6.0, ((0, 16),), jnp.float32),
    }


COEFS = (-205.0 / 72.0, 8.0 / 5.0, -1.0 / 5.0, 8.0 / 315.0, -1.0 / 560.0)
DAMP = 1.0

def laplace(wavefield):
    levels = wavefield.shape[-3]
    row_count = wavefield.shape[-2] - 8
    column_count = wavefield.shape[-1] - 8
    padding = [(0, 0)] * (wavefield.ndim - 3) + [(4, 4), (0, 0), (0, 0)]
    padded = jnp.pad(wavefield, padding)
    summed = 3.0 * COEFS[0] * wavefield[..., 4:4 + row_count, 4:4 + column_count]
    for offset in range(1, 5):
        neighbours = wavefield[..., 4 + offset:4 + offset + row_count, 4:4 + column_count] + wavefield[..., 4 - offset:4 - offset + row_count, 4:4 + column_count] + wavefield[..., 4:4 + row_count, 4 + offset:4 + offset + column_count] + wavefield[..., 4:4 + row_count, 4 - offset:4 - offset + column_count] + padded[..., 4 + offset:4 + offset + levels, 4:4 + row_count, 4:4 + column_count] + padded[..., 4 - offset:4 - offset + levels, 4:4 + row_count, 4:4 + column_count]
        summed = summed + COEFS[offset] * neighbours
    return summed

def injection(anchor_x, anchor_y, extent_x, extent_y, where_x, where_y, weights):
    cells_x = anchor_x + jnp.arange(extent_x, dtype=jnp.int32)
    cells_y = anchor_y + jnp.arange(extent_y, dtype=jnp.int32)
    left_hot = (where_x[:, None] == cells_x[None, :]).astype(jnp.float32) * weights[:, None]
    right_hot = (where_y[:, None] == cells_y[None, :]).astype(jnp.float32)
    return jnp.einsum('ra,rb->ab', left_hot, right_hot, precision=lax.Precision.HIGHEST)

def advance(current, previous, lap_now, speed_sq, born_dir, damp, source_plane, receiver_plane, counts, level_mask):
    drive = jnp.stack([level_mask * source_plane, born_dir * lap_now[0], level_mask * receiver_plane, born_dir * lap_now[2] + level_mask * counts * current[1]])
    return (2.0 * current - (1.0 - damp) * previous + speed_sq * lap_now + drive) / (1.0 + damp)

def reference(fields_now, fields_before, speed_sq, born_dir, pml_x, pml_y, src_x, src_y, src_amp, rec_x, rec_y, residual):
    level_mask = (jnp.arange(NZ) == 1).astype(jnp.float32)[:, None, None]
    layer_x = pml_x.astype(jnp.float32) / PML_W
    layer_y = pml_y.astype(jnp.float32) / PML_W
    damp = DAMP * (layer_x[:, None] * layer_x[:, None] + layer_y[None, :] * layer_y[None, :])
    grad_sum = jnp.zeros((NZ, NX, NY), jnp.float32)
    hess_sum = jnp.zeros((NZ, NX, NY), jnp.float32)
    finals = []
    ones_rec = jnp.ones((NREC,), jnp.float32)
    for shot_index in range(SHOTS):
        current = fields_now[shot_index]
        previous = fields_before[shot_index]
        counts = injection(0, 0, NX, NY, rec_x[shot_index], rec_y[shot_index], ones_rec)
        for turn in range(2):
            padded = jnp.pad(current, ((0, 0), (0, 0), (4, 4), (4, 4)))
            lap_now = laplace(padded)
            source_plane = injection(0, 0, NX, NY, src_x[shot_index:shot_index + 1], src_y[shot_index:shot_index + 1], src_amp[shot_index, turn:turn + 1])
            receiver_plane = injection(0, 0, NX, NY, rec_x[shot_index], rec_y[shot_index], residual[shot_index, turn])
            grad_sum = grad_sum + current[2] * lap_now[0]
            hess_sum = hess_sum + current[3] * lap_now[0] + current[2] * lap_now[1]
            stepped = advance(current, previous, lap_now, speed_sq, born_dir, damp, source_plane, receiver_plane, counts, level_mask)
            previous = current
            current = stepped
        finals.append(current)
    gradient = grad_sum / SHOTS
    hess_vec = hess_sum / SHOTS
    curvature = jnp.sum(born_dir * hess_vec) / math.sqrt(NZ * NX * NY)
    return (jnp.stack(finals), gradient, hess_vec, curvature)
```

```python
import functools
import math

import jax
import jax.numpy as jnp
from jax import lax
from jax.experimental import pallas as pl
from jax.experimental.pallas import tpu as pltpu
from jax.sharding import PartitionSpec as P

PML_W = 16
COEFS = (-205.0 / 72.0, 8.0 / 5.0, -1.0 / 5.0, 8.0 / 315.0, -1.0 / 560.0)
LEVELS = 8
ROWS = 64
COLS = 128
BLOCKS = ROWS // 8
MESH = pl.DeviceIdType.MESH


def kernel(
    sizes,
    now_ref,
    before_ref,
    speed_ref,
    born_ref,
    pml_x_ref,
    pml_y_ref,
    src_x_ref,
    src_y_ref,
    amp_ref,
    rec_x_ref,
    rec_y_ref,
    res_ref,
    out_ref,
    sums_ref,
    curv_ref,
    field0,
    field1,
    prev,
    speed,
    born,
    terms,
    sib,
    up_sum,
    down_sum,
    x_send,
    x_recv,
    y_send,
    y_recv,
    merged,
    planes,
    curv_sib,
    curv_y,
    curv_x,
    curv_z,
    in_sems,
    x_sems,
    y_sems,
    out_sem,
    sib_sems,
    rs_sems,
    ag_sems,
    agsib_sems,
    cs_sems,
    cy_sems,
    cx_sems,
    cz_sems,
):
    shots, n_x, n_y = sizes
    n_z = shots // 2
    reach = n_z // 2
    per = LEVELS // n_z
    shot = lax.axis_index("shot")
    core = lax.rem(shot, 2)
    z = shot // 2
    gx = lax.axis_index("gx")
    gy = lax.axis_index("gy")

    def z_id(k):
        return {"shot": lax.rem(z + k + 2 * n_z, n_z) * 2 + core}

    def x_id(k):
        return {"gx": lax.rem(gx + k + n_x, n_x)}

    def y_id(k):
        return {"gy": lax.rem(gy + k + n_y, n_y)}

    sib_id = {"shot": 2 * z + 1 - core}

    def remote(src, dst, send, recv, who):
        return pltpu.make_async_remote_copy(
            src_ref=src, dst_ref=dst, send_sem=send, recv_sem=recv, device_id=who, device_id_type=MESH
        )

    loads = [
        pltpu.make_async_copy(now_ref.at[0], field0.at[:, :, pl.ds(8, ROWS), :], in_sems.at[0]),
        pltpu.make_async_copy(before_ref.at[0], prev, in_sems.at[1]),
        pltpu.make_async_copy(speed_ref, speed, in_sems.at[2]),
        pltpu.make_async_copy(born_ref, born, in_sems.at[3]),
    ]
    for load in loads:
        load.start()

    barrier = pltpu.get_barrier_semaphore()
    partners = [sib_id]
    partners += [z_id(k) for k in range(1, n_z)]
    partners += [x_id(k) for k in range(1, n_x)]
    partners += [y_id(k) for k in range(1, n_y)]
    for who in partners:
        pl.semaphore_signal(barrier, inc=1, device_id=who, device_id_type=MESH)

    row0 = gx * ROWS
    col0 = gy * COLS
    whole_x = n_x * ROWS
    whole_y = n_y * COLS
    row = row0 + lax.broadcasted_iota(jnp.int32, (ROWS, COLS), 0)
    col = col0 + lax.broadcasted_iota(jnp.int32, (ROWS, COLS), 1)

    def layer(place, length, far):
        value = jnp.maximum(jnp.maximum(PML_W - place, far - (length - 1 - place)), 0)
        return value.astype(jnp.float32) / PML_W

    layer_x = layer(row, whole_x, pml_x_ref[whole_x - 1])
    layer_y = layer(col, whole_y, pml_y_ref[whole_y - 1])
    damp = layer_x * layer_x + layer_y * layer_y
    inverse = 1.0 / (1.0 + damp)
    planes[0] = inverse
    planes[1] = (1.0 - damp) * inverse
    at_source = (row == src_x_ref[0]) & (col == src_y_ref[0])
    planes[2] = jnp.where(at_source, amp_ref[0, 0], 0.0)
    planes[3] = jnp.where(at_source, amp_ref[0, 1], 0.0)
    count_rec = rec_x_ref.shape[1]
    hot_x = rec_x_ref[...] == row0 + lax.broadcasted_iota(jnp.int32, (ROWS, count_rec), 0)
    hot_y = rec_y_ref[...] == col0 + lax.broadcasted_iota(jnp.int32, (COLS, count_rec), 0)
    weights = [jnp.ones((1, count_rec), jnp.float32)]
    for turn in range(2):
        rest = res_ref[0, turn : turn + 1, :]
        for _ in range(3):
            head = rest.astype(jnp.bfloat16).astype(jnp.float32)
            weights.append(head)
            rest = rest - head
    left = jnp.concatenate([jnp.where(hot_x, w, 0.0).astype(jnp.bfloat16) for w in weights], axis=0)
    right = jnp.where(hot_y, 1.0, 0.0).astype(jnp.bfloat16)
    hits = lax.dot_general(
        left, right, (((1,), (1,)), ((), ())), preferred_element_type=jnp.float32
    )
    parts = [hits[i * ROWS : (i + 1) * ROWS] for i in range(7)]
    planes[4] = parts[1] + parts[2] + parts[3]
    planes[5] = parts[4] + parts[5] + parts[6]
    planes[6] = parts[0]

    lane = lax.broadcasted_iota(jnp.int32, (8, COLS), 1)
    low_half = (lane & 4) == 0
    group = lane // 8

    def block(b):
        return pl.ds(pl.multiple_of(b * 8, 8), 8)

    def inner(b, shift=0):
        return pl.ds(pl.multiple_of(b * 8, 8) + (8 + shift), 8)

    def pack_x(field):
        for f in range(4):
            for lev in range(LEVELS):
                x_send[0, f * 8 + lev] = field[f, lev, 8:12, :]
                x_send[1, f * 8 + lev] = field[f, lev, ROWS + 4 : ROWS + 8, :]

    def pack_y(field):
        def body(b, carry):
            packed = []
            for pair in range(2):
                total = jnp.zeros((8, COLS), jnp.float32)
                for i in range(16):
                    value = field[2 * pair + i // 8, i % 8, inner(b), :]
                    rolled = pltpu.roll(value, (8 * i + 4) % COLS, 1)
                    total = jnp.where(group == i, rolled, total)
                packed.append(total)
            y_send[0, block(b), :] = jnp.where(low_half, packed[0], pltpu.roll(packed[1], 4, 1))
            y_send[1, block(b), :] = jnp.where(low_half, pltpu.roll(packed[0], COLS - 4, 1), packed[1])
            return carry

        lax.fori_loop(0, BLOCKS, body, 0)

    def halo_copies(turn):
        return [
            remote(x_send.at[0], x_recv.at[turn, 0], x_sems.at[0, turn, 0], x_sems.at[1, turn, 0], x_id(-1)),
            remote(x_send.at[1], x_recv.at[turn, 1], x_sems.at[0, turn, 1], x_sems.at[1, turn, 1], x_id(1)),
            remote(y_send.at[0], y_recv.at[turn, 0], y_sems.at[0, turn, 0], y_sems.at[1, turn, 0], y_id(1)),
            remote(y_send.at[1], y_recv.at[turn, 1], y_sems.at[0, turn, 1], y_sems.at[1, turn, 1], y_id(-1)),
        ]

    def unpack(field, turn):
        for f in range(4):
            for lev in range(LEVELS):
                below = x_recv[turn, 0, f * 8 + lev]
                above = x_recv[turn, 1, f * 8 + lev]
                field[f, lev, 4:8, :] = jnp.where(gx == 0, 0.0, above)
                field[f, lev, ROWS + 8 : ROWS + 12, :] = jnp.where(gx == n_x - 1, 0.0, below)
        for b in range(BLOCKS):
            rows = pl.ds(b * 8, 8)
            tails = jnp.where(gy == 0, 0.0, y_recv[turn, 0, rows, :])
            heads = jnp.where(gy == n_y - 1, 0.0, y_recv[turn, 1, rows, :])
            merged[0, rows, :] = jnp.where(low_half, heads, pltpu.roll(tails, COLS - 4, 1))
            merged[1, rows, :] = jnp.where(
                low_half, pltpu.roll(heads, COLS - 4, 1), pltpu.roll(tails, COLS - 8, 1)
            )

    def laplace(field, f, b, centre, sides):
        results = []
        for lev in range(LEVELS):
            own = centre[lev]
            at = (8 * (f % 2) + lev) * 8
            side = pltpu.roll(sides, (COLS - at) % COLS, 1) if at else sides
            total = (3.0 * COEFS[0]) * own
            for k in range(1, 5):
                near = field[f, lev, inner(b, k), :] + field[f, lev, inner(b, -k), :]
                near += pltpu.roll(jnp.where(lane < k, side, own), COLS - k, 1)
                near += pltpu.roll(jnp.where(lane >= COLS - k, side, own), k, 1)
                if lev + k < LEVELS:
                    near += centre[lev + k]
                if lev - k >= 0:
                    near += centre[lev - k]
                total += COEFS[k] * near
            results.append(total)
        return results

    def old(turn, f, lev, b):
        return prev[f, lev, block(b), :] if turn == 0 else field0[f, lev, inner(b), :]

    def put(turn, f, lev, b, value):
        if turn == 0:
            field1[f, lev, inner(b), :] = value
        else:
            prev[f, lev, block(b), :] = value

    def incident(turn, field):
        def body(b, curv):
            sides = merged[0, block(b), :]
            u = [field[0, lev, inner(b), :] for lev in range(LEVELS)]
            du = [field[1, lev, inner(b), :] for lev in range(LEVELS)]
            lap_u = laplace(field, 0, b, u, sides)
            lap_du = laplace(field, 1, b, du, sides)
            inv = planes[0, block(b), :]
            fade = planes[1, block(b), :]
            for lev in range(LEVELS):
                lam = field[2, lev, inner(b), :]
                dlam = field[3, lev, inner(b), :]
                grad = lam * lap_u[lev]
                hess = dlam * lap_u[lev] + lam * lap_du[lev]
                if turn == 1:
                    grad += terms[0, lev, block(b), :]
                    hess += terms[1, lev, block(b), :]
                terms[0, lev, block(b), :] = grad
                terms[1, lev, block(b), :] = hess
                direction = born[lev, block(b), :]
                if turn == 1:
                    curv += direction * hess
                pace = speed[lev, block(b), :]
                new_u = 2.0 * u[lev] + pace * lap_u[lev]
                if lev == 1:
                    new_u += planes[2 + turn, block(b), :]
                new_du = 2.0 * du[lev] + pace * lap_du[lev] + direction * lap_u[lev]
                put(turn, 0, lev, b, new_u * inv - fade * old(turn, 0, lev, b))
                put(turn, 1, lev, b, new_du * inv - fade * old(turn, 1, lev, b))
            return curv

        return lax.fori_loop(0, BLOCKS, body, jnp.zeros((8, COLS), jnp.float32))

    def adjoint(turn, field):
        def body(b, carry):
            sides = merged[1, block(b), :]
            lam = [field[2, lev, inner(b), :] for lev in range(LEVELS)]
            dlam = [field[3, lev, inner(b), :] for lev in range(LEVELS)]
            lap_lam = laplace(field, 2, b, lam, sides)
            lap_dlam = laplace(field, 3, b, dlam, sides)
            inv = planes[0, block(b), :]
            fade = planes[1, block(b), :]
            for lev in range(LEVELS):
                pace = speed[lev, block(b), :]
                new_lam = 2.0 * lam[lev] + pace * lap_lam[lev]
                new_dlam = 2.0 * dlam[lev] + pace * lap_dlam[lev] + born[lev, block(b), :] * lap_lam[lev]
                if lev == 1:
                    new_lam += planes[4 + turn, block(b), :]
                    new_dlam += planes[6, block(b), :] * field[1, lev, inner(b), :]
                put(turn, 2, lev, b, new_lam * inv - fade * old(turn, 2, lev, b))
                put(turn, 3, lev, b, new_dlam * inv - fade * old(turn, 3, lev, b))
            return carry

        lax.fori_loop(0, BLOCKS, body, 0)

    loads[0].wait()
    pack_y(field0)
    pack_x(field0)
    pl.semaphore_wait(barrier, len(partners))
    copies = halo_copies(0)
    for copy in copies:
        copy.start()
    for load in loads[1:]:
        load.wait()
    for copy in copies:
        copy.wait()
    unpack(field0, 0)
    incident(0, field0)
    adjoint(0, field0)

    pack_y(field1)
    pack_x(field1)
    copies = halo_copies(1)
    for copy in copies:
        copy.start()
    for copy in copies:
        copy.wait()
    unpack(field1, 1)
    curv = incident(1, field1)

    swap = remote(terms.at[1 - core], sib, sib_sems.at[0], sib_sems.at[1], sib_id)
    swap.start()
    curv_sib[core] = curv
    curv_swap = remote(curv_sib.at[core], curv_sib.at[core], cs_sems.at[0], cs_sems.at[1], sib_id)
    curv_swap.start()

    def spread(buffer, place, value, sems, ident, count):
        buffer[place] = value
        sent = [
            remote(buffer.at[place], buffer.at[place], sems.at[0, k - 1], sems.at[1, k - 1], ident(k))
            for k in range(1, count)
        ]
        for copy in sent:
            copy.start()
        return sent

    def gather(sent, buffer, count):
        for copy in sent:
            copy.wait()
        total = buffer[0]
        for k in range(1, count):
            total = total + buffer[k]
        return total

    curv_swap.wait()
    curv = curv_sib[0] + curv_sib[1]
    sent_y = spread(curv_x, gx, curv, cx_sems, x_id, n_x)

    adjoint(1, field1)
    save = pltpu.make_async_copy(prev, out_ref.at[0], out_sem)
    save.start()

    def owner(k):
        return pl.ds(lax.rem(z + k + 2 * n_z, n_z) * per, per)

    halves = (pl.ds(0, ROWS // 2), pl.ds(ROWS // 2, ROWS // 2))
    full = pl.ds(0, ROWS)
    sums = (up_sum, down_sum)
    signs = (1, -1)

    def add(level, rows, *others):
        total = terms[core, level, rows, :]
        for other in others:
            total = total + other
        terms[core, level, rows, :] = total

    swap.wait()
    sent = []
    waiting = [None, None]
    for way in range(2):
        level = owner(reach)
        add(level, halves[way], sib[level, halves[way], :])
        copy = remote(
            terms.at[core, level, halves[way], :],
            sums[way].at[0, :, halves[way], :],
            rs_sems.at[0, way, 0],
            rs_sems.at[1, way, 0],
            z_id(signs[way]),
        )
        copy.start()
        waiting[way] = copy
        sent.append(copy)
    for k in range(1, reach):
        for way in range(2):
            level = owner(signs[way] * k)
            add(level, full, sib[level, full, :])
    add(owner(0), full, sib[owner(0), full, :])
    for step in range(1, reach):
        for way in range(2):
            waiting[way].wait_recv()
            rows = halves[way] if step == 1 else full
            level = owner(signs[way] * (reach - step))
            add(level, rows, sums[way][step - 1, :, rows, :])
            copy = remote(
                terms.at[core, level, full, :],
                sums[way].at[step, :, full, :],
                rs_sems.at[0, way, step],
                rs_sems.at[1, way, step],
                z_id(signs[way]),
            )
            copy.start()
            waiting[way] = copy
            sent.append(copy)
        if step == 1:
            curv = gather(sent_y, curv_x, n_x)
            sent_x = spread(curv_y, gy, curv, cy_sems, y_id, n_y)
        if step == 2:
            curv = gather(sent_x, curv_y, n_y)
            sent_z = spread(curv_z, z, curv, cz_sems, z_id, n_z)
    if reach == 1:
        curv = gather(sent_y, curv_x, n_x)
        sent_x = spread(curv_y, gy, curv, cy_sems, y_id, n_y)
    if reach <= 2:
        curv = gather(sent_x, curv_y, n_y)
        sent_z = spread(curv_z, z, curv, cz_sems, z_id, n_z)
    for way in range(2):
        waiting[way].wait_recv()
        rows = halves[way] if reach == 1 else full
        add(owner(0), rows, sums[way][reach - 1, :, rows, :])
    for copy in sent:
        copy.wait_send()
    sums_ref[core, owner(0)] = terms[core, owner(0)] * (1.0 / shots)

    sent = []
    across = []

    def to_sibling(level, rows, slot):
        copy = remote(
            sums_ref.at[core, level, rows, :],
            sums_ref.at[core, level, rows, :],
            agsib_sems.at[0, slot],
            agsib_sems.at[1, slot],
            sib_id,
        )
        copy.start()
        across.append(copy)

    for step in range(reach):
        for way in range(2):
            if step:
                waiting[way].wait_recv()
            rows = halves[way] if step == reach - 1 else full
            level = owner(-signs[way] * step)
            copy = remote(
                sums_ref.at[core, level, rows, :],
                sums_ref.at[core, level, rows, :],
                ag_sems.at[0, way, step],
                ag_sems.at[1, way, step],
                z_id(signs[way]),
            )
            copy.start()
            waiting[way] = copy
            sent.append(copy)
        if step == 0:
            to_sibling(owner(0), full, 0)
        else:
            for way in range(2):
                to_sibling(owner(-signs[way] * step), full, 2 * step - 1 + way)
    curv = gather(sent_z, curv_z, n_z)
    cells = LEVELS * whole_x * whole_y
    curv_ref[0, 0] = jnp.sum(curv) * (1.0 / (shots * math.sqrt(cells)))
    for way in range(2):
        waiting[way].wait_recv()
        to_sibling(owner(reach), halves[way], 2 * reach - 1 + way)
    for copy in sent:
        copy.wait_send()
    for copy in across:
        copy.wait()
    save.wait()


def local(sizes, *args):
    shots, n_x, n_y = sizes
    n_z = shots // 2
    reach = n_z // 2
    per = LEVELS // n_z
    any_space = pl.BlockSpec(memory_space=pl.ANY)
    smem = pl.BlockSpec(memory_space=pltpu.SMEM)
    vmem = pl.BlockSpec(memory_space=pltpu.VMEM)
    f32 = jnp.float32
    dma = pltpu.SemaphoreType.DMA
    tile = (8, COLS)
    fields, sums, curv = pl.pallas_call(
        functools.partial(kernel, sizes),
        out_shape=(
            jax.ShapeDtypeStruct((1, 4, LEVELS, ROWS, COLS), f32),
            jax.ShapeDtypeStruct((2, LEVELS, ROWS, COLS), f32),
            jax.ShapeDtypeStruct((1, 1), f32),
        ),
        in_specs=[any_space] * 4 + [smem] * 5 + [vmem] * 3,
        out_specs=(any_space, vmem, smem),
        scratch_shapes=[
            pltpu.VMEM((4, LEVELS, ROWS + 16, COLS), f32),
            pltpu.VMEM((4, LEVELS, ROWS + 16, COLS), f32),
            pltpu.VMEM((4, LEVELS, ROWS, COLS), f32),
            pltpu.VMEM((LEVELS, ROWS, COLS), f32),
            pltpu.VMEM((LEVELS, ROWS, COLS), f32),
            pltpu.VMEM((2, LEVELS, ROWS, COLS), f32),
            pltpu.VMEM((LEVELS, ROWS, COLS), f32),
            pltpu.VMEM((reach, per, ROWS, COLS), f32),
            pltpu.VMEM((reach, per, ROWS, COLS), f32),
            pltpu.VMEM((2, 32, 4, COLS), f32),
            pltpu.VMEM((2, 2, 32, 4, COLS), f32),
            pltpu.VMEM((2, ROWS, COLS), f32),
            pltpu.VMEM((2, 2, ROWS, COLS), f32),
            pltpu.VMEM((2, ROWS, COLS), f32),
            pltpu.VMEM((7, ROWS, COLS), f32),
            pltpu.VMEM((2,) + tile, f32),
            pltpu.VMEM((n_y,) + tile, f32),
            pltpu.VMEM((n_x,) + tile, f32),
            pltpu.VMEM((n_z,) + tile, f32),
            dma((4,)),
            dma((2, 2, 2)),
            dma((2, 2, 2)),
            dma,
            dma((2,)),
            dma((2, 2, reach)),
            dma((2, 2, reach)),
            dma((2, 2 * reach + 1)),
            dma((2,)),
            dma((2, n_y - 1)),
            dma((2, n_x - 1)),
            dma((2, n_z - 1)),
        ],
        compiler_params=pltpu.CompilerParams(
            collective_id=0, has_side_effects=True, vmem_limit_bytes=32 * 1024 * 1024
        ),
    )(*args)
    return fields, sums[0], sums[1], curv[0, 0]


def solution(mesh):
    sizes = (mesh.shape["shot"], mesh.shape["gx"], mesh.shape["gy"])
    placed = (
        P("shot", None, None, "gx", "gy"),
        P("shot", None, None, "gx", "gy"),
        P(None, "gx", "gy"),
        P(None, "gx", "gy"),
        P(),
        P(),
        P("shot"),
        P("shot"),
        P("shot", None),
        P("shot", None),
        P("shot", None),
        P("shot", None, None),
    )
    return jax.shard_map(
        functools.partial(local, sizes),
        mesh=mesh,
        in_specs=placed,
        out_specs=(
            P("shot", None, None, "gx", "gy"),
            P(None, "gx", "gy"),
            P(None, "gx", "gy"),
            P(),
        ),
        check_vma=False,
    )
```

```python
import functools
import math

import jax
import jax.numpy as jnp
import ml_dtypes
import numpy as np
from jax import lax
from jax.experimental import pallas as pl
from jax.experimental.pallas import tpu as pltpu
from jax.sharding import PartitionSpec as P

PML_W = 16
COEFS = (-205.0 / 72.0, 8.0 / 5.0, -1.0 / 5.0, 8.0 / 315.0, -1.0 / 560.0)
LEVELS = 8
ROWS = 64
COLS = 128
BLOCKS = ROWS // 8
MESH = pl.DeviceIdType.MESH


def rounded(value):
    return float(np.asarray(value, ml_dtypes.bfloat16))


HEADS = tuple(rounded(c) for c in COEFS)
RESTS = tuple(rounded(c - h) for c, h in zip(COEFS, HEADS))


def kernel(
    sizes,
    now_ref,
    before_ref,
    speed_ref,
    born_ref,
    pml_x_ref,
    pml_y_ref,
    src_x_ref,
    src_y_ref,
    amp_ref,
    rec_x_ref,
    rec_y_ref,
    res_ref,
    out_ref,
    sums_ref,
    curv_ref,
    field0,
    field1,
    prev,
    speed,
    born,
    terms,
    sib,
    lap,
    band,
    corner,
    join,
    direct,
    x_send,
    x_recv,
    y_send,
    y_recv,
    edge,
    sides,
    planes,
    curv_sib,
    curv_y,
    curv_x,
    curv_z,
    far_x,
    far_y,
    at_x,
    at_y,
    pulse,
    recs_x,
    recs_y,
    weigh,
    in_sems,
    small_sems,
    x_sems,
    y_sems,
    out_sem,
    sib_sems,
    rs_sems,
    ag_sems,
    agsib_sems,
    last_sems,
    cs_sems,
    cy_sems,
    cx_sems,
    cz_sems,
):
    shots, n_x, n_y = sizes
    n_z = shots // 2
    reach = n_z // 2
    per = LEVELS // n_z
    shot = lax.axis_index("shot")
    core = lax.rem(shot, 2)
    z = shot // 2
    gx = lax.axis_index("gx")
    gy = lax.axis_index("gy")

    def z_id(k):
        return {"shot": lax.rem(z + k + 2 * n_z, n_z) * 2 + core}

    def cross_id(k):
        return {"shot": lax.rem(z + k + 2 * n_z, n_z) * 2 + 1 - core}

    def x_id(k):
        return {"gx": lax.rem(gx + k + n_x, n_x)}

    def y_id(k):
        return {"gy": lax.rem(gy + k + n_y, n_y)}

    sib_id = {"shot": 2 * z + 1 - core}

    def remote(src, dst, send, recv, who):
        return pltpu.make_async_remote_copy(
            src_ref=src, dst_ref=dst, send_sem=send, recv_sem=recv, device_id=who, device_id_type=MESH
        )

    loads = [
        pltpu.make_async_copy(now_ref.at[0], field0.at[:, :, pl.ds(8, ROWS), :], in_sems.at[0]),
        pltpu.make_async_copy(before_ref.at[0], prev, in_sems.at[1]),
        pltpu.make_async_copy(speed_ref, speed, in_sems.at[2]),
        pltpu.make_async_copy(born_ref, born, in_sems.at[3]),
    ]
    small = [
        pltpu.make_async_copy(source, target, small_sems.at[i])
        for i, (source, target) in enumerate(
            [
                (pml_x_ref, far_x),
                (pml_y_ref, far_y),
                (src_x_ref, at_x),
                (src_y_ref, at_y),
                (amp_ref, pulse),
                (rec_x_ref, recs_x),
                (rec_y_ref, recs_y),
                (res_ref, weigh),
            ]
        )
    ]
    for load in [loads[0]] + small + loads[1:]:
        load.start()

    barrier = pltpu.get_barrier_semaphore()
    partners = [sib_id]
    partners += [z_id(k) for k in range(1, n_z)]
    partners += [cross_id(1), cross_id(-1)]
    partners += [x_id(k) for k in range(1, n_x)]
    partners += [y_id(k) for k in range(1, n_y)]
    for who in partners:
        pl.semaphore_signal(barrier, inc=1, device_id=who, device_id_type=MESH)

    whole_x = n_x * ROWS
    whole_y = n_y * COLS

    def build_planes():
        for load in small:
            load.wait()
        row0 = gx * ROWS
        col0 = gy * COLS
        row = row0 + lax.broadcasted_iota(jnp.int32, (ROWS, COLS), 0)
        col = col0 + lax.broadcasted_iota(jnp.int32, (ROWS, COLS), 1)

        def layer(place, length, far):
            value = jnp.maximum(jnp.maximum(PML_W - place, far - (length - 1 - place)), 0)
            return value.astype(jnp.float32) / PML_W

        layer_x = layer(row, whole_x, far_x[whole_x - 1])
        layer_y = layer(col, whole_y, far_y[whole_y - 1])
        damp = layer_x * layer_x + layer_y * layer_y
        inverse = 1.0 / (1.0 + damp)
        planes[0] = inverse
        planes[1] = (1.0 - damp) * inverse
        at_source = (row == at_x[0]) & (col == at_y[0])
        planes[2] = jnp.where(at_source, pulse[0, 0], 0.0)
        planes[3] = jnp.where(at_source, pulse[0, 1], 0.0)
        count_rec = recs_x.shape[1]
        hot_x = recs_x[...] == row0 + lax.broadcasted_iota(jnp.int32, (ROWS, count_rec), 0)
        hot_y = recs_y[...] == col0 + lax.broadcasted_iota(jnp.int32, (COLS, count_rec), 0)
        weights = [jnp.ones((1, count_rec), jnp.float32)]
        for turn in range(2):
            rest = weigh[0, turn : turn + 1, :]
            for _ in range(3):
                head = rest.astype(jnp.bfloat16).astype(jnp.float32)
                weights.append(head)
                rest = rest - head
        left = jnp.concatenate([jnp.where(hot_x, w, 0.0).astype(jnp.bfloat16) for w in weights], axis=0)
        right = jnp.where(hot_y, 1.0, 0.0).astype(jnp.bfloat16)
        hits = lax.dot_general(
            left, right, (((1,), (1,)), ((), ())), preferred_element_type=jnp.float32
        )
        parts = [hits[i * ROWS : (i + 1) * ROWS] for i in range(7)]
        planes[4] = parts[1] + parts[2] + parts[3]
        planes[5] = parts[4] + parts[5] + parts[6]
        planes[6] = parts[0]

    lane = lax.broadcasted_iota(jnp.int32, (8, COLS), 1)
    low_half = (lane & 4) == 0
    group = lane // 8

    def build_weights():
        shape = (2 * COLS, 2 * COLS)
        row = lax.broadcasted_iota(jnp.int32, shape, 0)
        col = lax.broadcasted_iota(jnp.int32, shape, 1)
        second = col >= COLS
        row = row & (COLS - 1)
        col = col & (COLS - 1)
        away = jnp.abs(row - col)
        ahead = (col - row) & (COLS - 1)
        ahead = jnp.where((row & 4) != 0, ahead, COLS - ahead)
        crosses = (row & 4) != (col & 4)
        near = jnp.zeros(shape, jnp.float32)
        far = jnp.zeros(shape, jnp.float32)
        for k in range(1, 5):
            value = jnp.where(second, RESTS[k], HEADS[k])
            near = jnp.where(away == k, value, near)
            far = jnp.where((ahead == k) & crosses, value, far)
        band[...] = near.astype(jnp.bfloat16)
        corner[...] = far.astype(jnp.bfloat16)

    def times(values, weights):
        head = values.astype(jnp.bfloat16)
        rest = (values - head.astype(jnp.float32)).astype(jnp.bfloat16)
        both = jnp.dot(
            jnp.concatenate([head, rest], axis=1), weights[...], preferred_element_type=jnp.float32
        )
        return both[:, :COLS] + both[:, COLS:]

    def block(b):
        return pl.ds(pl.multiple_of(b * 8, 8), 8)

    def inner(b, shift=0):
        return pl.ds(pl.multiple_of(b * 8, 8) + (8 + shift), 8)

    def pack_x(field):
        for f in range(4):
            for lev in range(LEVELS):
                x_send[0, f * 8 + lev] = field[f, lev, 8:12, :]
                x_send[1, f * 8 + lev] = field[f, lev, ROWS + 4 : ROWS + 8, :]

    def pack_y(field):
        def body(b, carry):
            packed = []
            for pair in range(2):
                total = jnp.zeros((8, COLS), jnp.float32)
                for i in range(16):
                    value = field[2 * pair + i // 8, i % 8, inner(b), :]
                    rolled = pltpu.roll(value, (8 * i + 4) % COLS, 1)
                    total = jnp.where(group == i, rolled, total)
                packed.append(total)
            y_send[0, block(b), :] = jnp.where(low_half, packed[0], pltpu.roll(packed[1], 4, 1))
            y_send[1, block(b), :] = jnp.where(low_half, pltpu.roll(packed[0], COLS - 4, 1), packed[1])
            return carry

        lax.fori_loop(0, BLOCKS, body, 0)

    def halo_copies(turn):
        return [
            remote(x_send.at[0], x_recv.at[turn, 0], x_sems.at[0, turn, 0], x_sems.at[1, turn, 0], x_id(-1)),
            remote(x_send.at[1], x_recv.at[turn, 1], x_sems.at[0, turn, 1], x_sems.at[1, turn, 1], x_id(1)),
            remote(y_send.at[0], y_recv.at[turn, 0], y_sems.at[0, turn, 0], y_sems.at[1, turn, 0], y_id(1)),
            remote(y_send.at[1], y_recv.at[turn, 1], y_sems.at[0, turn, 1], y_sems.at[1, turn, 1], y_id(-1)),
        ]

    def inside(field):
        def along_y(f, carry):
            values = field[f, :, 8 : 8 + ROWS, :].reshape(LEVELS * ROWS, COLS)
            lap[f] = times(values, band).reshape(LEVELS, ROWS, COLS)
            return carry

        lax.fori_loop(0, 4, along_y, 0)

        def along_xz(b, carry):
            for f in range(4):
                centre = [field[f, lev, inner(b), :] for lev in range(LEVELS)]
                for lev in range(LEVELS):
                    total = lap[f, lev, block(b), :] + (3.0 * COEFS[0]) * centre[lev]
                    for k in range(1, 5):
                        near = field[f, lev, inner(b, k), :] + field[f, lev, inner(b, -k), :]
                        if lev + k < LEVELS:
                            near += centre[lev + k]
                        if lev - k >= 0:
                            near += centre[lev - k]
                        total += COEFS[k] * near
                    lap[f, lev, block(b), :] = total
            return carry

        lax.fori_loop(0, BLOCKS, along_xz, 0)

    def unpack_y(turn):
        tails = jnp.where(gy == 0, 0.0, y_recv[turn, 0])
        heads = jnp.where(gy == n_y - 1, 0.0, y_recv[turn, 1])
        low = (lax.broadcasted_iota(jnp.int32, (ROWS, COLS), 1) & 4) == 0
        first = jnp.where(low, heads, pltpu.roll(tails, COLS - 4, 1))
        second = jnp.where(low, pltpu.roll(heads, COLS - 4, 1), pltpu.roll(tails, COLS - 8, 1))
        sides[...] = times(jnp.concatenate([first, second], axis=0), corner).reshape(2, ROWS, COLS)

    def unpack_x(turn):
        def body(f, carry):
            for lev in range(LEVELS):
                i = f * LEVELS + lev
                edge[0, i, 4:8, :] = jnp.where(gx == 0, 0.0, x_recv[turn, 1, i])
                edge[1, i, 8:12, :] = jnp.where(gx == n_x - 1, 0.0, x_recv[turn, 0, i])
            for lev in range(LEVELS):
                i = f * LEVELS + lev
                top = lap[f, lev, 0:8, :]
                bottom = lap[f, lev, ROWS - 8 : ROWS, :]
                for k in range(1, 5):
                    top += COEFS[k] * edge[0, i, 8 - k : 16 - k, :]
                    bottom += COEFS[k] * edge[1, i, k : k + 8, :]
                lap[f, lev, 0:8, :] = top
                lap[f, lev, ROWS - 8 : ROWS, :] = bottom
            return carry

        lax.fori_loop(0, 4, body, 0)

    outer = (lane < 4) | (lane >= COLS - 4)

    def laplace(f, b):
        side = sides[f // 2, block(b), :]
        results = []
        for lev in range(LEVELS):
            at = (8 * (f % 2) + lev) * 8
            turned = pltpu.roll(side, COLS - at, 1) if at else side
            results.append(lap[f, lev, block(b), :] + jnp.where(outer, turned, 0.0))
        return results

    def old(turn, f, lev, b):
        return prev[f, lev, block(b), :] if turn == 0 else field0[f, lev, inner(b), :]

    def put(turn, f, lev, b, value):
        if turn == 0:
            field1[f, lev, inner(b), :] = value
        else:
            prev[f, lev, block(b), :] = value

    def incident(turn, field):
        def body(b, curv):
            u = [field[0, lev, inner(b), :] for lev in range(LEVELS)]
            du = [field[1, lev, inner(b), :] for lev in range(LEVELS)]
            lap_u = laplace(0, b)
            lap_du = laplace(1, b)
            inv = planes[0, block(b), :]
            fade = planes[1, block(b), :]
            for lev in range(LEVELS):
                lam = field[2, lev, inner(b), :]
                dlam = field[3, lev, inner(b), :]
                grad = lam * lap_u[lev]
                hess = dlam * lap_u[lev] + lam * lap_du[lev]
                if turn == 1:
                    grad += terms[0, lev, block(b), :]
                    hess += terms[1, lev, block(b), :]
                terms[0, lev, block(b), :] = grad
                terms[1, lev, block(b), :] = hess
                direction = born[lev, block(b), :]
                if turn == 1:
                    curv += direction * hess
                pace = speed[lev, block(b), :]
                new_u = 2.0 * u[lev] + pace * lap_u[lev]
                if lev == 1:
                    new_u += planes[2 + turn, block(b), :]
                new_du = 2.0 * du[lev] + pace * lap_du[lev] + direction * lap_u[lev]
                put(turn, 0, lev, b, new_u * inv - fade * old(turn, 0, lev, b))
                put(turn, 1, lev, b, new_du * inv - fade * old(turn, 1, lev, b))
            return curv

        return lax.fori_loop(0, BLOCKS, body, jnp.zeros((8, COLS), jnp.float32))

    def adjoint(turn, field):
        def body(b, carry):
            lam = [field[2, lev, inner(b), :] for lev in range(LEVELS)]
            dlam = [field[3, lev, inner(b), :] for lev in range(LEVELS)]
            lap_lam = laplace(2, b)
            lap_dlam = laplace(3, b)
            inv = planes[0, block(b), :]
            fade = planes[1, block(b), :]
            for lev in range(LEVELS):
                pace = speed[lev, block(b), :]
                new_lam = 2.0 * lam[lev] + pace * lap_lam[lev]
                new_dlam = 2.0 * dlam[lev] + pace * lap_dlam[lev] + born[lev, block(b), :] * lap_lam[lev]
                if lev == 1:
                    new_lam += planes[4 + turn, block(b), :]
                    new_dlam += planes[6, block(b), :] * field[1, lev, inner(b), :]
                put(turn, 2, lev, b, new_lam * inv - fade * old(turn, 2, lev, b))
                put(turn, 3, lev, b, new_dlam * inv - fade * old(turn, 3, lev, b))
            return carry

        lax.fori_loop(0, BLOCKS, body, 0)

    def step_halos(field, turn, greet):
        pack_x(field)
        if greet:
            pl.semaphore_wait(barrier, len(partners))
        copies = halo_copies(turn)
        for copy in copies[:2]:
            copy.start()
        pack_y(field)
        for copy in copies[2:]:
            copy.start()
        return copies

    for field in (field0, field1):
        for f in range(4):
            for lev in range(LEVELS):
                field[f, lev, 0:8, :] = jnp.zeros((8, COLS), jnp.float32)
                field[f, lev, ROWS + 8 : ROWS + 16, :] = jnp.zeros((8, COLS), jnp.float32)
    for i in range(32):
        edge[0, i, 0:8, :] = jnp.zeros((8, COLS), jnp.float32)
        edge[0, i, 8:16, :] = jnp.zeros((8, COLS), jnp.float32)
        edge[1, i, 0:8, :] = jnp.zeros((8, COLS), jnp.float32)
        edge[1, i, 8:16, :] = jnp.zeros((8, COLS), jnp.float32)
    loads[0].wait()
    copies = step_halos(field0, 0, True)
    build_weights()
    build_planes()
    inside(field0)
    for load in loads[1:]:
        load.wait()
    for copy in copies[2:]:
        copy.wait()
    unpack_y(0)
    for copy in copies[:2]:
        copy.wait()
    unpack_x(0)
    incident(0, field0)
    adjoint(0, field0)

    copies = step_halos(field1, 1, False)
    inside(field1)
    for copy in copies[2:]:
        copy.wait()
    unpack_y(1)
    for copy in copies[:2]:
        copy.wait()
    unpack_x(1)
    curv = incident(1, field1)

    swap = remote(terms.at[1 - core], sib, sib_sems.at[0], sib_sems.at[1], sib_id)
    swap.start()
    curv_sib[core] = curv
    curv_swap = remote(curv_sib.at[core], curv_sib.at[core], cs_sems.at[0], cs_sems.at[1], sib_id)
    curv_swap.start()
    adjoint(1, field1)
    save = pltpu.make_async_copy(prev, out_ref.at[0], out_sem)
    save.start()

    def spread(buffer, place, value, sems, ident, count):
        buffer[place] = value
        sent = [
            remote(buffer.at[place], buffer.at[place], sems.at[0, k - 1], sems.at[1, k - 1], ident(k))
            for k in range(1, count)
        ]
        for copy in sent:
            copy.start()
        return sent

    def gather(sent, buffer, count):
        for copy in sent:
            copy.wait()
        total = buffer[0]
        for k in range(1, count):
            total = total + buffer[k]
        return total

    def owner(k):
        return pl.ds(lax.rem(z + k + 2 * n_z, n_z) * per, per)

    halves = (pl.ds(0, ROWS // 2), pl.ds(ROWS // 2, ROWS // 2))
    full = pl.ds(0, ROWS)
    signs = (1, -1)

    def add(level, rows, *others):
        total = terms[core, level, rows, :]
        for other in others:
            total = total + other
        terms[core, level, rows, :] = total

    def share(way, k):
        copy = remote(
            terms.at[core, owner(signs[way] * k), full, :],
            direct.at[way, k - 1],
            rs_sems.at[0, way, k],
            rs_sems.at[1, way, k],
            z_id(signs[way] * k),
        )
        copy.start()
        return copy

    swap.wait()
    joins = []
    for way in range(2):
        level = owner(reach)
        rows = halves[way]
        add(level, rows, sib[level, rows, :])
        copy = remote(
            terms.at[core, level, rows, :],
            join.at[way, :, rows, :],
            rs_sems.at[0, way, 0],
            rs_sems.at[1, way, 0],
            z_id(signs[way]),
        )
        copy.start()
        joins.append(copy)
    shares = []
    for k in range(reach - 2, 0, -1):
        for way in range(2):
            level = owner(signs[way] * k)
            add(level, full, sib[level, full, :])
            shares.append(share(way, k))
    curv_swap.wait()
    curv = curv_sib[0] + curv_sib[1]
    sent_y = spread(curv_x, gx, curv, cx_sems, x_id, n_x)
    for way in range(2):
        level = owner(signs[way] * (reach - 1))
        add(level, full, sib[level, full, :])
    add(owner(0), full, sib[owner(0), full, :])
    for way in range(2):
        joins[way].wait_recv()
        level = owner(signs[way] * (reach - 1))
        add(level, halves[way], join[way, :, halves[way], :])
        shares.append(share(way, reach - 1))
    curv = gather(sent_y, curv_x, n_x)
    sent_x = spread(curv_y, gy, curv, cy_sems, y_id, n_y)
    for copy in shares:
        copy.wait_recv()
    total = terms[core, owner(0)]
    for way in range(2):
        for k in range(1, reach):
            total = total + direct[way, k - 1]
    sums_ref[core, owner(0)] = total * (1.0 / shots)

    def pass_on(level, rows, pair, who):
        copy = remote(
            sums_ref.at[core, level, rows, :],
            sums_ref.at[core, level, rows, :],
            pair.at[0],
            pair.at[1],
            who,
        )
        copy.start()
        return copy

    spreads = {}
    for k in range(reach - 1, 0, -1):
        for way in range(2):
            spreads[way, k] = pass_on(
                owner(0), full, ag_sems.at[way, k - 1], z_id(signs[way] * k)
            )
    across = [pass_on(owner(0), full, agsib_sems.at[0], sib_id)]
    for copy in joins + shares:
        copy.wait_send()
    curv = gather(sent_x, curv_y, n_y)
    sent_z = spread(curv_z, z, curv, cz_sems, z_id, n_z)
    lasts = []
    for k in range(1, reach):
        for way in range(2):
            spreads[way, k].wait_recv()
            level = owner(-signs[way] * k)
            if k == reach - 1:
                lasts.append(pass_on(level, halves[way], last_sems.at[way, 0], z_id(signs[way])))
                lasts.append(pass_on(level, halves[way], last_sems.at[way, 1], cross_id(signs[way])))
            across.append(pass_on(level, full, agsib_sems.at[2 * k - 1 + way], sib_id))
    curv = gather(sent_z, curv_z, n_z)
    cells = LEVELS * whole_x * whole_y
    curv_ref[0, 0] = jnp.sum(curv) * (1.0 / (shots * math.sqrt(cells)))
    for copy in spreads.values():
        copy.wait_send()
    save.wait()
    for copy in across + lasts:
        copy.wait()


def local(sizes, *args):
    shots, n_x, n_y = sizes
    n_z = shots // 2
    reach = n_z // 2
    per = LEVELS // n_z
    any_space = pl.BlockSpec(memory_space=pl.ANY)
    smem = pl.BlockSpec(memory_space=pltpu.SMEM)
    vmem = pl.BlockSpec(memory_space=pltpu.VMEM)
    f32 = jnp.float32
    dma = pltpu.SemaphoreType.DMA
    tile = (8, COLS)
    fields, sums, curv = pl.pallas_call(
        functools.partial(kernel, sizes),
        out_shape=(
            jax.ShapeDtypeStruct((1, 4, LEVELS, ROWS, COLS), f32),
            jax.ShapeDtypeStruct((2, LEVELS, ROWS, COLS), f32),
            jax.ShapeDtypeStruct((1, 1), f32),
        ),
        in_specs=[any_space] * 12,
        out_specs=(any_space, vmem, smem),
        scratch_shapes=[
            pltpu.VMEM((4, LEVELS, ROWS + 16, COLS), f32),
            pltpu.VMEM((4, LEVELS, ROWS + 16, COLS), f32),
            pltpu.VMEM((4, LEVELS, ROWS, COLS), f32),
            pltpu.VMEM((LEVELS, ROWS, COLS), f32),
            pltpu.VMEM((LEVELS, ROWS, COLS), f32),
            pltpu.VMEM((2, LEVELS, ROWS, COLS), f32),
            pltpu.VMEM((LEVELS, ROWS, COLS), f32),
            pltpu.VMEM((4, LEVELS, ROWS, COLS), f32),
            pltpu.VMEM((2 * COLS, 2 * COLS), jnp.bfloat16),
            pltpu.VMEM((2 * COLS, 2 * COLS), jnp.bfloat16),
            pltpu.VMEM((2, per, ROWS, COLS), f32),
            pltpu.VMEM((2, reach - 1, per, ROWS, COLS), f32),
            pltpu.VMEM((2, 32, 4, COLS), f32),
            pltpu.VMEM((2, 2, 32, 4, COLS), f32),
            pltpu.VMEM((2, ROWS, COLS), f32),
            pltpu.VMEM((2, 2, ROWS, COLS), f32),
            pltpu.VMEM((2, 32, 16, COLS), f32),
            pltpu.VMEM((2, ROWS, COLS), f32),
            pltpu.VMEM((7, ROWS, COLS), f32),
            pltpu.VMEM((2,) + tile, f32),
            pltpu.VMEM((n_y,) + tile, f32),
            pltpu.VMEM((n_x,) + tile, f32),
            pltpu.VMEM((n_z,) + tile, f32),
            pltpu.SMEM(args[4].shape, jnp.int32),
            pltpu.SMEM(args[5].shape, jnp.int32),
            pltpu.SMEM(args[6].shape, jnp.int32),
            pltpu.SMEM(args[7].shape, jnp.int32),
            pltpu.SMEM(args[8].shape, f32),
            pltpu.VMEM(args[9].shape, jnp.int32),
            pltpu.VMEM(args[10].shape, jnp.int32),
            pltpu.VMEM(args[11].shape, f32),
            dma((4,)),
            dma((8,)),
            dma((2, 2, 2)),
            dma((2, 2, 2)),
            dma,
            dma((2,)),
            dma((2, 2, reach)),
            dma((2, reach - 1, 2)),
            dma((2 * reach - 1, 2)),
            dma((2, 2, 2)),
            dma((2,)),
            dma((2, n_y - 1)),
            dma((2, n_x - 1)),
            dma((2, n_z - 1)),
        ],
        compiler_params=pltpu.CompilerParams(
            collective_id=0, has_side_effects=True, vmem_limit_bytes=60 * 1024 * 1024
        ),
    )(*args)
    return fields, sums[0], sums[1], curv[0, 0]


def solution(mesh):
    sizes = (mesh.shape["shot"], mesh.shape["gx"], mesh.shape["gy"])
    placed = (
        P("shot", None, None, "gx", "gy"),
        P("shot", None, None, "gx", "gy"),
        P(None, "gx", "gy"),
        P(None, "gx", "gy"),
        P(),
        P(),
        P("shot"),
        P("shot"),
        P("shot", None),
        P("shot", None),
        P("shot", None),
        P("shot", None, None),
    )
    return jax.shard_map(
        functools.partial(local, sizes),
        mesh=mesh,
        in_specs=placed,
        out_specs=(
            P("shot", None, None, "gx", "gy"),
            P(None, "gx", "gy"),
            P(None, "gx", "gy"),
            P(),
        ),
        check_vma=False,
    )
```

```python
import functools
import math

import jax
import jax.numpy as jnp
import ml_dtypes
import numpy as np
from jax import lax
from jax.experimental import pallas as pl
from jax.experimental.pallas import tpu as pltpu
from jax.sharding import PartitionSpec as P

PML_W = 16
COEFS = (-205.0 / 72.0, 8.0 / 5.0, -1.0 / 5.0, 8.0 / 315.0, -1.0 / 560.0)
LEVELS = 8
ROWS = 64
COLS = 128
BLOCKS = ROWS // 8
MESH = pl.DeviceIdType.MESH


def rounded(value):
    return float(np.asarray(value, ml_dtypes.bfloat16))


HEADS = tuple(rounded(c) for c in COEFS)
RESTS = tuple(rounded(c - h) for c, h in zip(COEFS, HEADS))


def kernel(
    sizes,
    now_ref,
    before_ref,
    speed_ref,
    born_ref,
    pml_x_ref,
    pml_y_ref,
    src_x_ref,
    src_y_ref,
    amp_ref,
    rec_x_ref,
    rec_y_ref,
    res_ref,
    out_ref,
    sums_ref,
    curv_ref,
    field0,
    field1,
    prev,
    speed,
    born,
    terms,
    sib,
    lap,
    band,
    corner,
    join,
    direct,
    x_send,
    x_recv,
    y_send,
    y_recv,
    packed,
    edge,
    sides,
    planes,
    curv_sib,
    curv_y,
    curv_x,
    curv_z,
    far_x,
    far_y,
    at_x,
    at_y,
    pulse,
    recs_x,
    recs_y,
    weigh,
    in_sems,
    small_sems,
    x_sems,
    y_sems,
    sib_sems,
    rs_sems,
    ag_sems,
    agsib_sems,
    last_sems,
    cs_sems,
    cy_sems,
    cx_sems,
    cz_sems,
):
    shots, n_x, n_y = sizes
    n_z = shots // 2
    reach = n_z // 2
    per = LEVELS // n_z
    shot = lax.axis_index("shot")
    core = lax.rem(shot, 2)
    z = shot // 2
    gx = lax.axis_index("gx")
    gy = lax.axis_index("gy")

    def z_id(k):
        return {"shot": lax.rem(z + k + 2 * n_z, n_z) * 2 + core}

    def cross_id(k):
        return {"shot": lax.rem(z + k + 2 * n_z, n_z) * 2 + 1 - core}

    def x_id(k):
        return {"gx": lax.rem(gx + k + n_x, n_x)}

    def y_id(k):
        return {"gy": lax.rem(gy + k + n_y, n_y)}

    sib_id = {"shot": 2 * z + 1 - core}

    def remote(src, dst, send, recv, who):
        return pltpu.make_async_remote_copy(
            src_ref=src, dst_ref=dst, send_sem=send, recv_sem=recv, device_id=who, device_id_type=MESH
        )

    loads = [
        pltpu.make_async_copy(
            now_ref.at[0, pl.ds(2 * pair, 2)],
            field0.at[pl.ds(2 * pair, 2), :, pl.ds(8, ROWS), :],
            in_sems.at[pair],
        )
        for pair in range(2)
    ] + [
        pltpu.make_async_copy(before_ref.at[0], prev, in_sems.at[2]),
        pltpu.make_async_copy(speed_ref, speed, in_sems.at[3]),
        pltpu.make_async_copy(born_ref, born, in_sems.at[4]),
    ]
    small = [
        pltpu.make_async_copy(source, target, small_sems.at[i])
        for i, (source, target) in enumerate(
            [
                (pml_x_ref, far_x),
                (pml_y_ref, far_y),
                (src_x_ref, at_x),
                (src_y_ref, at_y),
                (amp_ref, pulse),
                (rec_x_ref, recs_x),
                (rec_y_ref, recs_y),
                (res_ref, weigh),
            ]
        )
    ]
    for load in loads[:2] + small + loads[2:]:
        load.start()

    barrier = pltpu.get_barrier_semaphore()
    partners = [sib_id]
    partners += [z_id(k) for k in range(1, n_z)]
    partners += [cross_id(1), cross_id(-1)]
    partners += [x_id(k) for k in range(1, n_x)]
    partners += [y_id(k) for k in range(1, n_y)]
    for who in partners:
        pl.semaphore_signal(barrier, inc=1, device_id=who, device_id_type=MESH)

    whole_x = n_x * ROWS
    whole_y = n_y * COLS

    def build_planes():
        for load in small:
            load.wait()
        row0 = gx * ROWS
        col0 = gy * COLS
        row = row0 + lax.broadcasted_iota(jnp.int32, (ROWS, COLS), 0)
        col = col0 + lax.broadcasted_iota(jnp.int32, (ROWS, COLS), 1)

        def layer(place, length, far):
            value = jnp.maximum(jnp.maximum(PML_W - place, far - (length - 1 - place)), 0)
            return value.astype(jnp.float32) / PML_W

        layer_x = layer(row, whole_x, far_x[whole_x - 1])
        layer_y = layer(col, whole_y, far_y[whole_y - 1])
        damp = layer_x * layer_x + layer_y * layer_y
        inverse = 1.0 / (1.0 + damp)
        planes[0] = inverse
        planes[1] = (1.0 - damp) * inverse
        at_source = (row == at_x[0]) & (col == at_y[0])
        planes[2] = jnp.where(at_source, pulse[0, 0], 0.0)
        planes[3] = jnp.where(at_source, pulse[0, 1], 0.0)
        count_rec = recs_x.shape[1]
        hot_x = recs_x[...] == row0 + lax.broadcasted_iota(jnp.int32, (ROWS, count_rec), 0)
        hot_y = recs_y[...] == col0 + lax.broadcasted_iota(jnp.int32, (COLS, count_rec), 0)
        weights = [jnp.ones((1, count_rec), jnp.float32)]
        for turn in range(2):
            rest = weigh[0, turn : turn + 1, :]
            for _ in range(3):
                head = rest.astype(jnp.bfloat16).astype(jnp.float32)
                weights.append(head)
                rest = rest - head
        left = jnp.concatenate([jnp.where(hot_x, w, 0.0).astype(jnp.bfloat16) for w in weights], axis=0)
        right = jnp.where(hot_y, 1.0, 0.0).astype(jnp.bfloat16)
        hits = lax.dot_general(
            left, right, (((1,), (1,)), ((), ())), preferred_element_type=jnp.float32
        )
        parts = [hits[i * ROWS : (i + 1) * ROWS] for i in range(7)]
        planes[4] = parts[1] + parts[2] + parts[3]
        planes[5] = parts[4] + parts[5] + parts[6]
        planes[6] = parts[0]

    lane = lax.broadcasted_iota(jnp.int32, (8, COLS), 1)
    group = ((lane + 4) & (COLS - 1)) // 8

    def build_weights():
        shape = (2 * COLS, 2 * COLS)
        row = lax.broadcasted_iota(jnp.int32, shape, 0)
        col = lax.broadcasted_iota(jnp.int32, shape, 1)
        second = col >= COLS
        row = row & (COLS - 1)
        col = col & (COLS - 1)
        away = jnp.abs(row - col)
        ahead = (col - row) & (COLS - 1)
        ahead = jnp.where((row & 4) != 0, ahead, COLS - ahead)
        crosses = (row & 4) != (col & 4)
        near = jnp.zeros(shape, jnp.float32)
        far = jnp.zeros(shape, jnp.float32)
        for k in range(1, 5):
            value = jnp.where(second, RESTS[k], HEADS[k])
            near = jnp.where(away == k, value, near)
            far = jnp.where((ahead == k) & crosses, value, far)
        band[...] = near.astype(jnp.bfloat16)
        corner[...] = far.astype(jnp.bfloat16)

    def times(values, weights):
        head = values.astype(jnp.bfloat16)
        rest = (values - head.astype(jnp.float32)).astype(jnp.bfloat16)
        both = jnp.dot(
            jnp.concatenate([head, rest], axis=1), weights[...], preferred_element_type=jnp.float32
        )
        return both[:, :COLS] + both[:, COLS:]

    def block(b):
        return pl.ds(pl.multiple_of(b * 8, 8), 8)

    def inner(b, shift=0):
        return pl.ds(pl.multiple_of(b * 8, 8) + (8 + shift), 8)

    def pack_x(field, turn, pair):
        for i in range(16):
            f, lev = 2 * pair + i // LEVELS, i % LEVELS
            x_send[turn, pair, 0, i] = field[f, lev, 8:12, :]
            x_send[turn, pair, 1, i] = field[f, lev, ROWS + 4 : ROWS + 8, :]

    def borders(values):
        total = values[0]
        for i in range(1, 16):
            total = jnp.where(group == i, pltpu.roll(values[i], 8 * i, 1), total)
        return total

    def pack_y(field, pair):
        def body(b, carry):
            values = [field[2 * pair + i // LEVELS, i % LEVELS, inner(b), :] for i in range(16)]
            packed[pair, block(b), :] = borders(values)
            return carry

        lax.fori_loop(0, BLOCKS, body, 0)

    half_rows = ROWS // 2
    is_tail = (lax.broadcasted_iota(jnp.int32, (half_rows, COLS), 1) & 4) != 0

    def fold_y(turn, pair):
        first = packed[pair, 0:half_rows, :]
        second = packed[pair, half_rows:ROWS, :]
        y_send[turn, pair, 0] = jnp.where(is_tail, first, pltpu.roll(second, 4, 1))
        y_send[turn, pair, 1] = jnp.where(is_tail, pltpu.roll(second, COLS - 4, 1), first)

    def halos(buffer_out, buffer_in, sems, turn, pair, ident, ways):
        copies = [
            remote(
                buffer_out.at[turn, pair, way],
                buffer_in.at[turn, pair, way],
                sems.at[0, turn, pair, way],
                sems.at[1, turn, pair, way],
                ident(ways[way]),
            )
            for way in range(2)
        ]
        for copy in copies:
            copy.start()
        return copies

    def send_x(turn, pair):
        return halos(x_send, x_recv, x_sems, turn, pair, x_id, (-1, 1))

    def send_y(turn, pair):
        fold_y(turn, pair)
        return halos(y_send, y_recv, y_sems, turn, pair, y_id, (1, -1))

    def inside(field, pair):
        def along_y(f, carry):
            values = field[f, :, 8 : 8 + ROWS, :].reshape(LEVELS * ROWS, COLS)
            lap[f] = times(values, band).reshape(LEVELS, ROWS, COLS)
            return carry

        lax.fori_loop(2 * pair, 2 * pair + 2, along_y, 0)

        def along_xz(b, carry):
            for f in (2 * pair, 2 * pair + 1):
                centre = [field[f, lev, inner(b), :] for lev in range(LEVELS)]
                for lev in range(LEVELS):
                    total = lap[f, lev, block(b), :] + (3.0 * COEFS[0]) * centre[lev]
                    for k in range(1, 5):
                        near = field[f, lev, inner(b, k), :] + field[f, lev, inner(b, -k), :]
                        if lev + k < LEVELS:
                            near += centre[lev + k]
                        if lev - k >= 0:
                            near += centre[lev - k]
                        total += COEFS[k] * near
                    lap[f, lev, block(b), :] = total
            return carry

        lax.fori_loop(0, BLOCKS, along_xz, 0)

    def unpack_y(turn, pair):
        tails = jnp.where(gy == 0, 0.0, y_recv[turn, pair, 0])
        heads = jnp.where(gy == n_y - 1, 0.0, y_recv[turn, pair, 1])
        first = jnp.where(is_tail, tails, heads)
        second = jnp.where(is_tail, pltpu.roll(tails, COLS - 4, 1), pltpu.roll(heads, 4, 1))
        sides[pair] = times(jnp.concatenate([first, second], axis=0), corner)

    def unpack_x(turn, pair):
        def body(f, carry):
            for lev in range(LEVELS):
                i = f * LEVELS + lev
                mine = (f - 2 * pair) * LEVELS + lev
                edge[0, i, 4:8, :] = jnp.where(gx == 0, 0.0, x_recv[turn, pair, 1, mine])
                edge[1, i, 8:12, :] = jnp.where(gx == n_x - 1, 0.0, x_recv[turn, pair, 0, mine])
            for lev in range(LEVELS):
                i = f * LEVELS + lev
                top = lap[f, lev, 0:8, :]
                bottom = lap[f, lev, ROWS - 8 : ROWS, :]
                for k in range(1, 5):
                    top += COEFS[k] * edge[0, i, 8 - k : 16 - k, :]
                    bottom += COEFS[k] * edge[1, i, k : k + 8, :]
                lap[f, lev, 0:8, :] = top
                lap[f, lev, ROWS - 8 : ROWS, :] = bottom
            return carry

        lax.fori_loop(2 * pair, 2 * pair + 2, body, 0)

    outer = (lane < 4) | (lane >= COLS - 4)

    def laplace(f, b):
        side = sides[f // 2, block(b), :]
        results = []
        for lev in range(LEVELS):
            at = (8 * (f % 2) + lev) * 8
            turned = pltpu.roll(side, COLS - at, 1) if at else side
            results.append(lap[f, lev, block(b), :] + jnp.where(outer, turned, 0.0))
        return results

    def old(turn, f, lev, b):
        return prev[f, lev, block(b), :] if turn == 0 else field0[f, lev, inner(b), :]

    def finish(turn, pair, b, fresh):
        for i in range(16):
            f, lev = 2 * pair + i // LEVELS, i % LEVELS
            if turn == 0:
                field1[f, lev, inner(b), :] = fresh[i]
            else:
                out_ref[0, f, lev, block(b), :] = fresh[i]
        if turn == 0:
            packed[pair, block(b), :] = borders(fresh)

    def incident(turn, field):
        def body(b, curv):
            u = [field[0, lev, inner(b), :] for lev in range(LEVELS)]
            du = [field[1, lev, inner(b), :] for lev in range(LEVELS)]
            lap_u = laplace(0, b)
            lap_du = laplace(1, b)
            fresh = [None] * 16
            inv = planes[0, block(b), :]
            fade = planes[1, block(b), :]
            for lev in range(LEVELS):
                lam = field[2, lev, inner(b), :]
                dlam = field[3, lev, inner(b), :]
                grad = lam * lap_u[lev]
                hess = dlam * lap_u[lev] + lam * lap_du[lev]
                if turn == 1:
                    grad += terms[0, lev, block(b), :]
                    hess += terms[1, lev, block(b), :]
                terms[0, lev, block(b), :] = grad
                terms[1, lev, block(b), :] = hess
                direction = born[lev, block(b), :]
                if turn == 1:
                    curv += direction * hess
                pace = speed[lev, block(b), :]
                new_u = 2.0 * u[lev] + pace * lap_u[lev]
                if lev == 1:
                    new_u += planes[2 + turn, block(b), :]
                new_du = 2.0 * du[lev] + pace * lap_du[lev] + direction * lap_u[lev]
                fresh[lev] = new_u * inv - fade * old(turn, 0, lev, b)
                fresh[LEVELS + lev] = new_du * inv - fade * old(turn, 1, lev, b)
            finish(turn, 0, b, fresh)
            return curv

        return lax.fori_loop(0, BLOCKS, body, jnp.zeros((8, COLS), jnp.float32))

    def adjoint(turn, field):
        def body(b, carry):
            lam = [field[2, lev, inner(b), :] for lev in range(LEVELS)]
            dlam = [field[3, lev, inner(b), :] for lev in range(LEVELS)]
            lap_lam = laplace(2, b)
            lap_dlam = laplace(3, b)
            fresh = [None] * 16
            inv = planes[0, block(b), :]
            fade = planes[1, block(b), :]
            for lev in range(LEVELS):
                pace = speed[lev, block(b), :]
                new_lam = 2.0 * lam[lev] + pace * lap_lam[lev]
                new_dlam = 2.0 * dlam[lev] + pace * lap_dlam[lev] + born[lev, block(b), :] * lap_lam[lev]
                if lev == 1:
                    new_lam += planes[4 + turn, block(b), :]
                    new_dlam += planes[6, block(b), :] * field[1, lev, inner(b), :]
                fresh[lev] = new_lam * inv - fade * old(turn, 2, lev, b)
                fresh[LEVELS + lev] = new_dlam * inv - fade * old(turn, 3, lev, b)
            finish(turn, 1, b, fresh)
            return carry

        lax.fori_loop(0, BLOCKS, body, 0)

    for field in (field0, field1):
        for f in range(4):
            for lev in range(LEVELS):
                field[f, lev, 0:8, :] = jnp.zeros((8, COLS), jnp.float32)
                field[f, lev, ROWS + 8 : ROWS + 16, :] = jnp.zeros((8, COLS), jnp.float32)
    for i in range(32):
        edge[0, i, 0:8, :] = jnp.zeros((8, COLS), jnp.float32)
        edge[0, i, 8:16, :] = jnp.zeros((8, COLS), jnp.float32)
        edge[1, i, 0:8, :] = jnp.zeros((8, COLS), jnp.float32)
        edge[1, i, 8:16, :] = jnp.zeros((8, COLS), jnp.float32)
    x_copies = {}
    y_copies = {}
    for pair in range(2):
        loads[pair].wait()
        pack_x(field0, 0, pair)
        if pair == 0:
            pl.semaphore_wait(barrier, len(partners))
        x_copies[0, pair] = send_x(0, pair)
        pack_y(field0, pair)
        y_copies[0, pair] = send_y(0, pair)
    build_weights()
    build_planes()
    inside(field0, 0)
    inside(field0, 1)
    for load in loads[2:]:
        load.wait()

    def take(turn, pair):
        for copy in y_copies[turn, pair]:
            copy.wait_recv()
        unpack_y(turn, pair)
        for copy in x_copies[turn, pair]:
            copy.wait_recv()
        unpack_x(turn, pair)

    take(0, 0)
    incident(0, field0)
    pack_x(field1, 1, 0)
    x_copies[1, 0] = send_x(1, 0)
    y_copies[1, 0] = send_y(1, 0)
    take(0, 1)
    adjoint(0, field0)
    pack_x(field1, 1, 1)
    x_copies[1, 1] = send_x(1, 1)
    y_copies[1, 1] = send_y(1, 1)

    inside(field1, 0)
    inside(field1, 1)
    take(1, 0)
    curv = incident(1, field1)

    swap = remote(terms.at[1 - core], sib, sib_sems.at[0], sib_sems.at[1], sib_id)
    swap.start()
    curv_sib[core] = curv
    curv_swap = remote(curv_sib.at[core], curv_sib.at[core], cs_sems.at[0], cs_sems.at[1], sib_id)
    curv_swap.start()
    take(1, 1)
    adjoint(1, field1)
    for copies in list(x_copies.values()) + list(y_copies.values()):
        for copy in copies:
            copy.wait_send()

    def spread(buffer, place, value, sems, ident, count):
        buffer[place] = value
        sent = [
            remote(buffer.at[place], buffer.at[place], sems.at[0, k - 1], sems.at[1, k - 1], ident(k))
            for k in range(1, count)
        ]
        for copy in sent:
            copy.start()
        return sent

    def gather(sent, buffer, count):
        for copy in sent:
            copy.wait()
        total = buffer[0]
        for k in range(1, count):
            total = total + buffer[k]
        return total

    def owner(k):
        return pl.ds(lax.rem(z + k + 2 * n_z, n_z) * per, per)

    halves = (pl.ds(0, ROWS // 2), pl.ds(ROWS // 2, ROWS // 2))
    full = pl.ds(0, ROWS)
    signs = (1, -1)

    def add(level, rows, *others):
        total = terms[core, level, rows, :]
        for other in others:
            total = total + other
        terms[core, level, rows, :] = total

    def share(way, k):
        copy = remote(
            terms.at[core, owner(signs[way] * k), full, :],
            direct.at[way, k - 1],
            rs_sems.at[0, way, k],
            rs_sems.at[1, way, k],
            z_id(signs[way] * k),
        )
        copy.start()
        return copy

    swap.wait()
    joins = []
    for way in range(2):
        level = owner(reach)
        rows = halves[way]
        add(level, rows, sib[level, rows, :])
        copy = remote(
            terms.at[core, level, rows, :],
            join.at[way, :, rows, :],
            rs_sems.at[0, way, 0],
            rs_sems.at[1, way, 0],
            z_id(signs[way]),
        )
        copy.start()
        joins.append(copy)
    shares = []
    for k in range(reach - 2, 0, -1):
        for way in range(2):
            level = owner(signs[way] * k)
            add(level, full, sib[level, full, :])
            shares.append(share(way, k))
    curv_swap.wait()
    curv = curv_sib[0] + curv_sib[1]
    sent_y = spread(curv_x, gx, curv, cx_sems, x_id, n_x)
    for way in range(2):
        level = owner(signs[way] * (reach - 1))
        add(level, full, sib[level, full, :])
    add(owner(0), full, sib[owner(0), full, :])
    for way in range(2):
        joins[way].wait_recv()
        level = owner(signs[way] * (reach - 1))
        add(level, halves[way], join[way, :, halves[way], :])
        shares.append(share(way, reach - 1))
    curv = gather(sent_y, curv_x, n_x)
    sent_x = spread(curv_y, gy, curv, cy_sems, y_id, n_y)
    for copy in shares:
        copy.wait_recv()
    total = terms[core, owner(0)]
    for way in range(2):
        for k in range(1, reach):
            total = total + direct[way, k - 1]
    sums_ref[core, owner(0)] = total * (1.0 / shots)

    def pass_on(level, rows, pair, who):
        copy = remote(
            sums_ref.at[core, level, rows, :],
            sums_ref.at[core, level, rows, :],
            pair.at[0],
            pair.at[1],
            who,
        )
        copy.start()
        return copy

    spreads = {}
    for k in range(reach - 1, 0, -1):
        for way in range(2):
            spreads[way, k] = pass_on(
                owner(0), full, ag_sems.at[way, k - 1], z_id(signs[way] * k)
            )
    across = [pass_on(owner(0), full, agsib_sems.at[0], sib_id)]
    for copy in joins + shares:
        copy.wait_send()
    curv = gather(sent_x, curv_y, n_y)
    sent_z = spread(curv_z, z, curv, cz_sems, z_id, n_z)
    lasts = []
    for k in range(1, reach):
        for way in range(2):
            spreads[way, k].wait_recv()
            level = owner(-signs[way] * k)
            if k == reach - 1:
                lasts.append(pass_on(level, halves[way], last_sems.at[way, 0], z_id(signs[way])))
                lasts.append(pass_on(level, halves[way], last_sems.at[way, 1], cross_id(signs[way])))
            across.append(pass_on(level, full, agsib_sems.at[2 * k - 1 + way], sib_id))
    curv = gather(sent_z, curv_z, n_z)
    cells = LEVELS * whole_x * whole_y
    curv_ref[...] = jnp.sum(curv, keepdims=True) * (1.0 / (shots * math.sqrt(cells)))
    for copy in spreads.values():
        copy.wait_send()
    for copy in across + lasts:
        copy.wait()


def deliver(fields_ref, sums_ref, curv_ref, out_ref, grad_ref, hess_ref, total_ref, sems):
    copies = [
        pltpu.make_async_copy(source, target, sems.at[i])
        for i, (source, target) in enumerate(
            [
                (fields_ref, out_ref),
                (sums_ref.at[0], grad_ref),
                (sums_ref.at[1], hess_ref),
                (curv_ref, total_ref),
            ]
        )
    ]
    for copy in copies:
        copy.start()
    for copy in copies:
        copy.wait()


def local(sizes, *args):
    shots, n_x, n_y = sizes
    n_z = shots // 2
    reach = n_z // 2
    per = LEVELS // n_z
    any_space = pl.BlockSpec(memory_space=pl.ANY)
    hbm = pl.BlockSpec(memory_space=pltpu.HBM)
    vmem = pl.BlockSpec(memory_space=pltpu.VMEM)
    f32 = jnp.float32
    dma = pltpu.SemaphoreType.DMA
    tile = (8, COLS)
    fields, sums, curv = pl.pallas_call(
        functools.partial(kernel, sizes),
        out_shape=(
            pltpu.VMEM((1, 4, LEVELS, ROWS, COLS), f32),
            pltpu.VMEM((2, LEVELS, ROWS, COLS), f32),
            pltpu.VMEM((1, 1), f32),
        ),
        in_specs=[any_space] * 12,
        out_specs=(vmem,) * 3,
        scratch_shapes=[
            pltpu.VMEM((4, LEVELS, ROWS + 16, COLS), f32),
            pltpu.VMEM((4, LEVELS, ROWS + 16, COLS), f32),
            pltpu.VMEM((4, LEVELS, ROWS, COLS), f32),
            pltpu.VMEM((LEVELS, ROWS, COLS), f32),
            pltpu.VMEM((LEVELS, ROWS, COLS), f32),
            pltpu.VMEM((2, LEVELS, ROWS, COLS), f32),
            pltpu.VMEM((LEVELS, ROWS, COLS), f32),
            pltpu.VMEM((4, LEVELS, ROWS, COLS), f32),
            pltpu.VMEM((2 * COLS, 2 * COLS), jnp.bfloat16),
            pltpu.VMEM((2 * COLS, 2 * COLS), jnp.bfloat16),
            pltpu.VMEM((2, per, ROWS, COLS), f32),
            pltpu.VMEM((2, reach - 1, per, ROWS, COLS), f32),
            pltpu.VMEM((2, 2, 2, 16, 4, COLS), f32),
            pltpu.VMEM((2, 2, 2, 16, 4, COLS), f32),
            pltpu.VMEM((2, 2, 2, ROWS // 2, COLS), f32),
            pltpu.VMEM((2, 2, 2, ROWS // 2, COLS), f32),
            pltpu.VMEM((2, ROWS, COLS), f32),
            pltpu.VMEM((2, 32, 16, COLS), f32),
            pltpu.VMEM((2, ROWS, COLS), f32),
            pltpu.VMEM((7, ROWS, COLS), f32),
            pltpu.VMEM((2,) + tile, f32),
            pltpu.VMEM((n_y,) + tile, f32),
            pltpu.VMEM((n_x,) + tile, f32),
            pltpu.VMEM((n_z,) + tile, f32),
            pltpu.SMEM(args[4].shape, jnp.int32),
            pltpu.SMEM(args[5].shape, jnp.int32),
            pltpu.SMEM((1,), jnp.int32),
            pltpu.SMEM((1,), jnp.int32),
            pltpu.SMEM(args[8].shape, f32),
            pltpu.VMEM(args[9].shape, jnp.int32),
            pltpu.VMEM(args[10].shape, jnp.int32),
            pltpu.VMEM(args[11].shape, f32),
            dma((5,)),
            dma((8,)),
            dma((2, 2, 2, 2)),
            dma((2, 2, 2, 2)),
            dma((2,)),
            dma((2, 2, reach)),
            dma((2, reach - 1, 2)),
            dma((2 * reach - 1, 2)),
            dma((2, 2, 2)),
            dma((2,)),
            dma((2, n_y - 1)),
            dma((2, n_x - 1)),
            dma((2, n_z - 1)),
        ],
        compiler_params=pltpu.CompilerParams(
            collective_id=0, has_side_effects=True, vmem_limit_bytes=32 * 1024 * 1024
        ),
    )(*[arg if arg.size == 1 else pltpu.with_memory_space_constraint(arg, pltpu.HBM) for arg in args])
    sums_shape = jax.ShapeDtypeStruct((LEVELS, ROWS, COLS), f32)
    fields, grad, hess, curv = pl.pallas_call(
        deliver,
        out_shape=(jax.ShapeDtypeStruct(fields.shape, f32), sums_shape, sums_shape, jax.ShapeDtypeStruct((1, 1), f32)),
        in_specs=[any_space] * 3,
        out_specs=(hbm,) * 4,
        scratch_shapes=[dma((4,))],
    )(*[pltpu.with_memory_space_constraint(value, pltpu.VMEM) for value in (fields, sums, curv)])
    return fields, grad, hess, curv[0, 0]


def solution(mesh):
    sizes = (mesh.shape["shot"], mesh.shape["gx"], mesh.shape["gy"])
    placed = (
        P("shot", None, None, "gx", "gy"),
        P("shot", None, None, "gx", "gy"),
        P(None, "gx", "gy"),
        P(None, "gx", "gy"),
        P(),
        P(),
        P("shot"),
        P("shot"),
        P("shot", None),
        P("shot", None),
        P("shot", None),
        P("shot", None, None),
    )
    return jax.shard_map(
        functools.partial(local, sizes),
        mesh=mesh,
        in_specs=placed,
        out_specs=(
            P("shot", None, None, "gx", "gy"),
            P(None, "gx", "gy"),
            P(None, "gx", "gy"),
            P(),
        ),
        check_vma=False,
    )
```

```python
import functools
import math

import jax
import jax.numpy as jnp
import ml_dtypes
import numpy as np
from jax import lax
from jax.experimental import pallas as pl
from jax.experimental.pallas import tpu as pltpu
from jax.sharding import PartitionSpec as P

PML_W = 16
COEFS = (-205.0 / 72.0, 8.0 / 5.0, -1.0 / 5.0, 8.0 / 315.0, -1.0 / 560.0)
LEVELS = 8
ROWS = 64
COLS = 128
BLOCKS = ROWS // 8
MESH = pl.DeviceIdType.MESH


def rounded(value):
    return float(np.asarray(value, ml_dtypes.bfloat16))


HEADS = tuple(rounded(c) for c in COEFS)
RESTS = tuple(rounded(c - h) for c, h in zip(COEFS, HEADS))


def kernel(
    sizes,
    now_ref,
    before_ref,
    speed_ref,
    born_ref,
    pml_x_ref,
    pml_y_ref,
    src_x_ref,
    src_y_ref,
    amp_ref,
    rec_x_ref,
    rec_y_ref,
    res_ref,
    out_ref,
    sums_ref,
    curv_ref,
    field0,
    field1,
    prev,
    speed,
    born,
    terms,
    sib,
    lap,
    band,
    corner,
    direct,
    x_send,
    x_recv,
    y_send,
    y_recv,
    packed,
    edge,
    sides,
    planes,
    curv_sib,
    curv_y,
    curv_x,
    curv_z,
    far_x,
    far_y,
    at_x,
    at_y,
    pulse,
    recs_x,
    recs_y,
    weigh,
    in_sems,
    small_sems,
    x_sems,
    y_sems,
    sib_sems,
    rs_sems,
    ag_sems,
    agsib_sems,
    cs_sems,
    cy_sems,
    cx_sems,
    cz_sems,
):
    shots, n_x, n_y = sizes
    n_z = shots // 2
    per = LEVELS // n_z
    shot = lax.axis_index("shot")
    core = lax.rem(shot, 2)
    z = shot // 2
    gx = lax.axis_index("gx")
    gy = lax.axis_index("gy")

    def z_id(k):
        return {"shot": lax.rem(z + k + 2 * n_z, n_z) * 2 + core}

    def x_id(k):
        return {"gx": lax.rem(gx + k + n_x, n_x)}

    def y_id(k):
        return {"gy": lax.rem(gy + k + n_y, n_y)}

    sib_id = {"shot": 2 * z + 1 - core}

    def remote(src, dst, send, recv, who):
        return pltpu.make_async_remote_copy(
            src_ref=src, dst_ref=dst, send_sem=send, recv_sem=recv, device_id=who, device_id_type=MESH
        )

    loads = [
        pltpu.make_async_copy(
            now_ref.at[0, pl.ds(2 * pair, 2)],
            field0.at[pl.ds(2 * pair, 2), :, pl.ds(8, ROWS), :],
            in_sems.at[pair],
        )
        for pair in range(2)
    ] + [
        pltpu.make_async_copy(before_ref.at[0], prev, in_sems.at[2]),
        pltpu.make_async_copy(speed_ref, speed, in_sems.at[3]),
        pltpu.make_async_copy(born_ref, born, in_sems.at[4]),
    ]
    small = [
        pltpu.make_async_copy(source, target, small_sems.at[i])
        for i, (source, target) in enumerate(
            [
                (pml_x_ref, far_x),
                (pml_y_ref, far_y),
                (src_x_ref, at_x),
                (src_y_ref, at_y),
                (amp_ref, pulse),
                (rec_x_ref, recs_x),
                (rec_y_ref, recs_y),
                (res_ref, weigh),
            ]
        )
    ]
    barrier = pltpu.get_barrier_semaphore()
    partners = [sib_id]
    partners += [z_id(k) for k in range(1, n_z)]
    partners += [x_id(k) for k in range(1, n_x)]
    partners += [y_id(k) for k in range(1, n_y)]
    for who in partners:
        pl.semaphore_signal(barrier, inc=1, device_id=who, device_id_type=MESH)

    for load in loads[:2] + small + loads[2:]:
        load.start()

    whole_x = n_x * ROWS
    whole_y = n_y * COLS

    def build_planes():
        for load in small:
            load.wait()
        row0 = gx * ROWS
        col0 = gy * COLS
        row = row0 + lax.broadcasted_iota(jnp.int32, (ROWS, COLS), 0)
        col = col0 + lax.broadcasted_iota(jnp.int32, (ROWS, COLS), 1)

        def layer(place, length, far):
            value = jnp.maximum(jnp.maximum(PML_W - place, far - (length - 1 - place)), 0)
            return value.astype(jnp.float32) / PML_W

        layer_x = layer(row, whole_x, far_x[whole_x - 1])
        layer_y = layer(col, whole_y, far_y[whole_y - 1])
        damp = layer_x * layer_x + layer_y * layer_y
        inverse = 1.0 / (1.0 + damp)
        planes[0] = inverse
        planes[1] = (1.0 - damp) * inverse
        at_source = (row == at_x[0]) & (col == at_y[0])
        planes[2] = jnp.where(at_source, pulse[0, 0], 0.0)
        planes[3] = jnp.where(at_source, pulse[0, 1], 0.0)
        count_rec = recs_x.shape[1]
        hot_x = recs_x[...] == row0 + lax.broadcasted_iota(jnp.int32, (ROWS, count_rec), 0)
        hot_y = recs_y[...] == col0 + lax.broadcasted_iota(jnp.int32, (COLS, count_rec), 0)
        weights = [jnp.ones((1, count_rec), jnp.float32)]
        for turn in range(2):
            rest = weigh[0, turn : turn + 1, :]
            for _ in range(3):
                head = rest.astype(jnp.bfloat16).astype(jnp.float32)
                weights.append(head)
                rest = rest - head
        left = jnp.concatenate([jnp.where(hot_x, w, 0.0).astype(jnp.bfloat16) for w in weights], axis=0)
        right = jnp.where(hot_y, 1.0, 0.0).astype(jnp.bfloat16)
        hits = lax.dot_general(
            left, right, (((1,), (1,)), ((), ())), preferred_element_type=jnp.float32
        )
        parts = [hits[i * ROWS : (i + 1) * ROWS] for i in range(7)]
        planes[4] = parts[1] + parts[2] + parts[3]
        planes[5] = parts[4] + parts[5] + parts[6]
        planes[6] = parts[0]

    lane = lax.broadcasted_iota(jnp.int32, (8, COLS), 1)
    group = ((lane + 4) & (COLS - 1)) // 8

    def build_weights():
        shape = (2 * COLS, 2 * COLS)
        row = lax.broadcasted_iota(jnp.int32, shape, 0)
        col = lax.broadcasted_iota(jnp.int32, shape, 1)
        second = col >= COLS
        row = row & (COLS - 1)
        col = col & (COLS - 1)
        away = jnp.abs(row - col)
        ahead = (col - row) & (COLS - 1)
        ahead = jnp.where((row & 4) != 0, ahead, COLS - ahead)
        crosses = (row & 4) != (col & 4)
        near = jnp.zeros(shape, jnp.float32)
        far = jnp.zeros(shape, jnp.float32)
        for k in range(1, 5):
            value = jnp.where(second, RESTS[k], HEADS[k])
            near = jnp.where(away == k, value, near)
            far = jnp.where((ahead == k) & crosses, value, far)
        band[...] = near.astype(jnp.bfloat16)
        corner[...] = far.astype(jnp.bfloat16)

    def times(values, weights):
        head = values.astype(jnp.bfloat16)
        rest = (values - head.astype(jnp.float32)).astype(jnp.bfloat16)
        both = jnp.dot(
            jnp.concatenate([head, rest], axis=1), weights[...], preferred_element_type=jnp.float32
        )
        return both[:, :COLS] + both[:, COLS:]

    def block(b):
        return pl.ds(pl.multiple_of(b * 8, 8), 8)

    def inner(b, shift=0):
        return pl.ds(pl.multiple_of(b * 8, 8) + (8 + shift), 8)

    def pack_x(field, turn, pair):
        for i in range(16):
            f, lev = 2 * pair + i // LEVELS, i % LEVELS
            x_send[turn, pair, 0, i] = field[f, lev, 8:12, :]
            x_send[turn, pair, 1, i] = field[f, lev, ROWS + 4 : ROWS + 8, :]

    def borders(values):
        total = values[0]
        for i in range(1, 16):
            total = jnp.where(group == i, pltpu.roll(values[i], 8 * i, 1), total)
        return total

    def pack_y(field, pair):
        def body(b, carry):
            values = [field[2 * pair + i // LEVELS, i % LEVELS, inner(b), :] for i in range(16)]
            packed[pair, block(b), :] = borders(values)
            return carry

        lax.fori_loop(0, BLOCKS, body, 0)

    half_rows = ROWS // 2
    is_tail = (lax.broadcasted_iota(jnp.int32, (half_rows, COLS), 1) & 4) != 0

    def fold_y(turn, pair):
        first = packed[pair, 0:half_rows, :]
        second = packed[pair, half_rows:ROWS, :]
        y_send[turn, pair, 0] = jnp.where(is_tail, first, pltpu.roll(second, 4, 1))
        y_send[turn, pair, 1] = jnp.where(is_tail, pltpu.roll(second, COLS - 4, 1), first)

    def halos(buffer_out, buffer_in, sems, turn, pair, ident, ways):
        copies = [
            remote(
                buffer_out.at[turn, pair, way],
                buffer_in.at[turn, pair, way],
                sems.at[0, turn, pair, way],
                sems.at[1, turn, pair, way],
                ident(ways[way]),
            )
            for way in range(2)
        ]
        for copy in copies:
            copy.start()
        return copies

    def send_x(turn, pair):
        return halos(x_send, x_recv, x_sems, turn, pair, x_id, (-1, 1))

    def send_y(turn, pair):
        fold_y(turn, pair)
        return halos(y_send, y_recv, y_sems, turn, pair, y_id, (1, -1))

    def inside(field, pair):
        def along_y(f, carry):
            values = field[f, :, 8 : 8 + ROWS, :].reshape(LEVELS * ROWS, COLS)
            lap[f] = times(values, band).reshape(LEVELS, ROWS, COLS)
            return carry

        lax.fori_loop(2 * pair, 2 * pair + 2, along_y, 0)

        def along_xz(b, carry):
            for f in (2 * pair, 2 * pair + 1):
                centre = [field[f, lev, inner(b), :] for lev in range(LEVELS)]
                for lev in range(LEVELS):
                    total = lap[f, lev, block(b), :] + (3.0 * COEFS[0]) * centre[lev]
                    for k in range(1, 5):
                        near = field[f, lev, inner(b, k), :] + field[f, lev, inner(b, -k), :]
                        if lev + k < LEVELS:
                            near += centre[lev + k]
                        if lev - k >= 0:
                            near += centre[lev - k]
                        total += COEFS[k] * near
                    lap[f, lev, block(b), :] = total
            return carry

        lax.fori_loop(0, BLOCKS, along_xz, 0)

    def unpack_y(turn, pair):
        tails = jnp.where(gy == 0, 0.0, y_recv[turn, pair, 0])
        heads = jnp.where(gy == n_y - 1, 0.0, y_recv[turn, pair, 1])
        first = jnp.where(is_tail, tails, heads)
        second = jnp.where(is_tail, pltpu.roll(tails, COLS - 4, 1), pltpu.roll(heads, 4, 1))
        sides[pair] = times(jnp.concatenate([first, second], axis=0), corner)

    def unpack_x(turn, pair):
        def body(f, carry):
            for lev in range(LEVELS):
                i = f * LEVELS + lev
                mine = (f - 2 * pair) * LEVELS + lev
                edge[0, i, 4:8, :] = jnp.where(gx == 0, 0.0, x_recv[turn, pair, 1, mine])
                edge[1, i, 8:12, :] = jnp.where(gx == n_x - 1, 0.0, x_recv[turn, pair, 0, mine])
            for lev in range(LEVELS):
                i = f * LEVELS + lev
                top = lap[f, lev, 0:8, :]
                bottom = lap[f, lev, ROWS - 8 : ROWS, :]
                for k in range(1, 5):
                    top += COEFS[k] * edge[0, i, 8 - k : 16 - k, :]
                    bottom += COEFS[k] * edge[1, i, k : k + 8, :]
                lap[f, lev, 0:8, :] = top
                lap[f, lev, ROWS - 8 : ROWS, :] = bottom
            return carry

        lax.fori_loop(2 * pair, 2 * pair + 2, body, 0)

    outer = (lane < 4) | (lane >= COLS - 4)

    def laplace(f, b):
        side = sides[f // 2, block(b), :]
        results = []
        for lev in range(LEVELS):
            at = (8 * (f % 2) + lev) * 8
            turned = pltpu.roll(side, COLS - at, 1) if at else side
            results.append(lap[f, lev, block(b), :] + jnp.where(outer, turned, 0.0))
        return results

    def old(turn, f, lev, b):
        return prev[f, lev, block(b), :] if turn == 0 else field0[f, lev, inner(b), :]

    def finish(turn, pair, b, fresh):
        for i in range(16):
            f, lev = 2 * pair + i // LEVELS, i % LEVELS
            if turn == 0:
                field1[f, lev, inner(b), :] = fresh[i]
            else:
                out_ref[0, f, lev, block(b), :] = fresh[i]
        if turn == 0:
            packed[pair, block(b), :] = borders(fresh)

    def incident(turn, field, first, last, curv):
        def body(b, curv):
            u = [field[0, lev, inner(b), :] for lev in range(LEVELS)]
            du = [field[1, lev, inner(b), :] for lev in range(LEVELS)]
            lap_u = laplace(0, b)
            lap_du = laplace(1, b)
            fresh = [None] * 16
            inv = planes[0, block(b), :]
            fade = planes[1, block(b), :]
            for lev in range(LEVELS):
                lam = field[2, lev, inner(b), :]
                dlam = field[3, lev, inner(b), :]
                grad = lam * lap_u[lev]
                hess = dlam * lap_u[lev] + lam * lap_du[lev]
                if turn == 1:
                    grad += terms[0, lev, block(b), :]
                    hess += terms[1, lev, block(b), :]
                terms[0, lev, block(b), :] = grad
                terms[1, lev, block(b), :] = hess
                direction = born[lev, block(b), :]
                if turn == 1:
                    curv += direction * hess
                pace = speed[lev, block(b), :]
                new_u = 2.0 * u[lev] + pace * lap_u[lev]
                if lev == 1:
                    new_u += planes[2 + turn, block(b), :]
                new_du = 2.0 * du[lev] + pace * lap_du[lev] + direction * lap_u[lev]
                fresh[lev] = new_u * inv - fade * old(turn, 0, lev, b)
                fresh[LEVELS + lev] = new_du * inv - fade * old(turn, 1, lev, b)
            finish(turn, 0, b, fresh)
            return curv

        return lax.fori_loop(first, last, body, curv)

    def adjoint(turn, field):
        def body(b, carry):
            lam = [field[2, lev, inner(b), :] for lev in range(LEVELS)]
            dlam = [field[3, lev, inner(b), :] for lev in range(LEVELS)]
            lap_lam = laplace(2, b)
            lap_dlam = laplace(3, b)
            fresh = [None] * 16
            inv = planes[0, block(b), :]
            fade = planes[1, block(b), :]
            for lev in range(LEVELS):
                pace = speed[lev, block(b), :]
                new_lam = 2.0 * lam[lev] + pace * lap_lam[lev]
                new_dlam = 2.0 * dlam[lev] + pace * lap_dlam[lev] + born[lev, block(b), :] * lap_lam[lev]
                if lev == 1:
                    new_lam += planes[4 + turn, block(b), :]
                    new_dlam += planes[6, block(b), :] * field[1, lev, inner(b), :]
                fresh[lev] = new_lam * inv - fade * old(turn, 2, lev, b)
                fresh[LEVELS + lev] = new_dlam * inv - fade * old(turn, 3, lev, b)
            finish(turn, 1, b, fresh)
            return carry

        lax.fori_loop(0, BLOCKS, body, 0)

    for field in (field0, field1):
        for f in range(4):
            for lev in range(LEVELS):
                field[f, lev, 0:8, :] = jnp.zeros((8, COLS), jnp.float32)
                field[f, lev, ROWS + 8 : ROWS + 16, :] = jnp.zeros((8, COLS), jnp.float32)
    for i in range(32):
        edge[0, i, 0:8, :] = jnp.zeros((8, COLS), jnp.float32)
        edge[0, i, 8:16, :] = jnp.zeros((8, COLS), jnp.float32)
        edge[1, i, 0:8, :] = jnp.zeros((8, COLS), jnp.float32)
        edge[1, i, 8:16, :] = jnp.zeros((8, COLS), jnp.float32)
    x_copies = {}
    y_copies = {}
    for pair in range(2):
        loads[pair].wait()
        pack_x(field0, 0, pair)
        if pair == 0:
            pl.semaphore_wait(barrier, len(partners))
        x_copies[0, pair] = send_x(0, pair)
        pack_y(field0, pair)
        y_copies[0, pair] = send_y(0, pair)
    build_weights()
    build_planes()
    inside(field0, 0)
    inside(field0, 1)
    for load in loads[2:]:
        load.wait()

    def take(turn, pair):
        for copy in y_copies[turn, pair]:
            copy.wait_recv()
        unpack_y(turn, pair)
        for copy in x_copies[turn, pair]:
            copy.wait_recv()
        unpack_x(turn, pair)

    take(0, 0)
    nothing = jnp.zeros((8, COLS), jnp.float32)
    incident(0, field0, 0, BLOCKS, nothing)
    pack_x(field1, 1, 0)
    x_copies[1, 0] = send_x(1, 0)
    y_copies[1, 0] = send_y(1, 0)
    take(0, 1)
    adjoint(0, field0)
    pack_x(field1, 1, 1)
    x_copies[1, 1] = send_x(1, 1)
    y_copies[1, 1] = send_y(1, 1)

    inside(field1, 0)
    inside(field1, 1)
    take(1, 0)

    halves = (pl.ds(0, ROWS // 2), pl.ds(ROWS // 2, ROWS // 2))
    swaps = []
    curv = nothing
    for part in range(2):
        curv = incident(1, field1, part * (BLOCKS // 2), (part + 1) * (BLOCKS // 2), curv)
        swap = remote(
            terms.at[1 - core, :, halves[part], :],
            sib.at[:, halves[part], :],
            sib_sems.at[0, part],
            sib_sems.at[1, part],
            sib_id,
        )
        swap.start()
        swaps.append(swap)
    curv_sib[core] = curv
    curv_swap = remote(curv_sib.at[core], curv_sib.at[core], cs_sems.at[0], cs_sems.at[1], sib_id)
    curv_swap.start()
    take(1, 1)

    def spread(buffer, place, value, sems, ident, count):
        buffer[place] = value
        sent = [
            remote(buffer.at[place], buffer.at[place], sems.at[0, k - 1], sems.at[1, k - 1], ident(k))
            for k in range(1, count)
        ]
        for copy in sent:
            copy.start()
        return sent

    def gather(sent, buffer, count):
        for copy in sent:
            copy.wait()
        total = buffer[0]
        for k in range(1, count):
            total = total + buffer[k]
        return total

    def owner(k):
        return pl.ds(lax.rem(z + k + 2 * n_z, n_z) * per, per)

    order = sorted(range(1, n_z), key=lambda k: -min(k, n_z - k))
    shares = {}
    for part in range(2):
        rows = halves[part]
        swaps[part].wait_recv()
        for k in order:
            level = owner(k)
            terms[core, level, rows, :] = terms[core, level, rows, :] + sib[level, rows, :]
            shares[part, k] = remote(
                terms.at[core, level, rows, :],
                direct.at[part, k - 1],
                rs_sems.at[0, part, k - 1],
                rs_sems.at[1, part, k - 1],
                z_id(k),
            )
            shares[part, k].start()
        if part == 0:
            curv_swap.wait()
            curv = curv_sib[0] + curv_sib[1]
            sent_y = spread(curv_x, gx, curv, cx_sems, x_id, n_x)
    adjoint(1, field1)

    def pass_on(level, rows, sems, part, k, who):
        copy = remote(
            sums_ref.at[core, level, rows, :],
            sums_ref.at[core, level, rows, :],
            sems.at[0, part, k],
            sems.at[1, part, k],
            who,
        )
        copy.start()
        return copy

    spreads = {}
    across = []
    for part in range(2):
        rows = halves[part]
        total = terms[core, owner(0), rows, :] + sib[owner(0), rows, :]
        for k in reversed(order):
            shares[part, k].wait_recv()
            total = total + direct[part, k - 1]
        sums_ref[core, owner(0), rows, :] = total * (1.0 / shots)
        for k in order:
            spreads[part, k] = pass_on(owner(0), rows, ag_sems, part, k - 1, z_id(k))
        across.append(pass_on(owner(0), rows, agsib_sems, part, 0, sib_id))
        if part == 0:
            curv = gather(sent_y, curv_x, n_x)
            sent_x = spread(curv_y, gy, curv, cy_sems, y_id, n_y)
    curv = gather(sent_x, curv_y, n_y)
    sent_z = spread(curv_z, z, curv, cz_sems, z_id, n_z)
    for part in range(2):
        for k in reversed(order):
            spreads[part, k].wait_recv()
            across.append(pass_on(owner(-k), halves[part], agsib_sems, part, k, sib_id))
    curv = gather(sent_z, curv_z, n_z)
    cells = LEVELS * whole_x * whole_y
    curv_ref[...] = jnp.sum(curv, keepdims=True) * (1.0 / (shots * math.sqrt(cells)))
    for copies in list(x_copies.values()) + list(y_copies.values()):
        for copy in copies:
            copy.wait_send()
    for copy in swaps + list(shares.values()) + list(spreads.values()):
        copy.wait_send()
    for copy in across:
        copy.wait()


def deliver(fields_ref, sums_ref, curv_ref, out_ref, grad_ref, hess_ref, total_ref, sems):
    copies = [
        pltpu.make_async_copy(source, target, sems.at[i])
        for i, (source, target) in enumerate(
            [
                (fields_ref, out_ref),
                (sums_ref.at[0], grad_ref),
                (sums_ref.at[1], hess_ref),
                (curv_ref, total_ref),
            ]
        )
    ]
    for copy in copies:
        copy.start()
    for copy in copies:
        copy.wait()


def local(sizes, *args):
    shots, n_x, n_y = sizes
    n_z = shots // 2
    per = LEVELS // n_z
    any_space = pl.BlockSpec(memory_space=pl.ANY)
    hbm = pl.BlockSpec(memory_space=pltpu.HBM)
    vmem = pl.BlockSpec(memory_space=pltpu.VMEM)
    f32 = jnp.float32
    dma = pltpu.SemaphoreType.DMA
    tile = (8, COLS)
    fields, sums, curv = pl.pallas_call(
        functools.partial(kernel, sizes),
        out_shape=(
            pltpu.VMEM((1, 4, LEVELS, ROWS, COLS), f32),
            pltpu.VMEM((2, LEVELS, ROWS, COLS), f32),
            pltpu.VMEM((1, 1), f32),
        ),
        in_specs=[any_space] * 12,
        out_specs=(vmem,) * 3,
        scratch_shapes=[
            pltpu.VMEM((4, LEVELS, ROWS + 16, COLS), f32),
            pltpu.VMEM((4, LEVELS, ROWS + 16, COLS), f32),
            pltpu.VMEM((4, LEVELS, ROWS, COLS), f32),
            pltpu.VMEM((LEVELS, ROWS, COLS), f32),
            pltpu.VMEM((LEVELS, ROWS, COLS), f32),
            pltpu.VMEM((2, LEVELS, ROWS, COLS), f32),
            pltpu.VMEM((LEVELS, ROWS, COLS), f32),
            pltpu.VMEM((4, LEVELS, ROWS, COLS), f32),
            pltpu.VMEM((2 * COLS, 2 * COLS), jnp.bfloat16),
            pltpu.VMEM((2 * COLS, 2 * COLS), jnp.bfloat16),
            pltpu.VMEM((2, n_z - 1, per, ROWS // 2, COLS), f32),
            pltpu.VMEM((2, 2, 2, 16, 4, COLS), f32),
            pltpu.VMEM((2, 2, 2, 16, 4, COLS), f32),
            pltpu.VMEM((2, 2, 2, ROWS // 2, COLS), f32),
            pltpu.VMEM((2, 2, 2, ROWS // 2, COLS), f32),
            pltpu.VMEM((2, ROWS, COLS), f32),
            pltpu.VMEM((2, 32, 16, COLS), f32),
            pltpu.VMEM((2, ROWS, COLS), f32),
            pltpu.VMEM((7, ROWS, COLS), f32),
            pltpu.VMEM((2,) + tile, f32),
            pltpu.VMEM((n_y,) + tile, f32),
            pltpu.VMEM((n_x,) + tile, f32),
            pltpu.VMEM((n_z,) + tile, f32),
            pltpu.SMEM(args[4].shape, jnp.int32),
            pltpu.SMEM(args[5].shape, jnp.int32),
            pltpu.SMEM((1,), jnp.int32),
            pltpu.SMEM((1,), jnp.int32),
            pltpu.SMEM(args[8].shape, f32),
            pltpu.VMEM(args[9].shape, jnp.int32),
            pltpu.VMEM(args[10].shape, jnp.int32),
            pltpu.VMEM(args[11].shape, f32),
            dma((5,)),
            dma((8,)),
            dma((2, 2, 2, 2)),
            dma((2, 2, 2, 2)),
            dma((2, 2)),
            dma((2, 2, n_z - 1)),
            dma((2, 2, n_z - 1)),
            dma((2, 2, n_z)),
            dma((2,)),
            dma((2, n_y - 1)),
            dma((2, n_x - 1)),
            dma((2, n_z - 1)),
        ],
        compiler_params=pltpu.CompilerParams(
            collective_id=0, has_side_effects=True, vmem_limit_bytes=32 * 1024 * 1024
        ),
    )(*[arg if arg.size == 1 else pltpu.with_memory_space_constraint(arg, pltpu.HBM) for arg in args])
    sums_shape = jax.ShapeDtypeStruct((LEVELS, ROWS, COLS), f32)
    fields, grad, hess, curv = pl.pallas_call(
        deliver,
        out_shape=(jax.ShapeDtypeStruct(fields.shape, f32), sums_shape, sums_shape, jax.ShapeDtypeStruct((1, 1), f32)),
        in_specs=[any_space] * 3,
        out_specs=(hbm,) * 4,
        scratch_shapes=[dma((4,))],
    )(*[pltpu.with_memory_space_constraint(value, pltpu.VMEM) for value in (fields, sums, curv)])
    return fields, grad, hess, curv[0, 0]


def solution(mesh):
    sizes = (mesh.shape["shot"], mesh.shape["gx"], mesh.shape["gy"])
    placed = (
        P("shot", None, None, "gx", "gy"),
        P("shot", None, None, "gx", "gy"),
        P(None, "gx", "gy"),
        P(None, "gx", "gy"),
        P(),
        P(),
        P("shot"),
        P("shot"),
        P("shot", None),
        P("shot", None),
        P("shot", None),
        P("shot", None, None),
    )
    return jax.shard_map(
        functools.partial(local, sizes),
        mesh=mesh,
        in_specs=placed,
        out_specs=(
            P("shot", None, None, "gx", "gy"),
            P(None, "gx", "gy"),
            P(None, "gx", "gy"),
            P(),
        ),
        check_vma=False,
    )
```

```python
import functools
import math

import jax
import jax.numpy as jnp
import ml_dtypes
import numpy as np
from jax import lax
from jax.experimental import pallas as pl
from jax.experimental.pallas import tpu as pltpu
from jax.sharding import PartitionSpec as P

PML_W = 16
COEFS = (-205.0 / 72.0, 8.0 / 5.0, -1.0 / 5.0, 8.0 / 315.0, -1.0 / 560.0)
LEVELS = 8
ROWS = 64
COLS = 128
BLOCKS = ROWS // 8
MESH = pl.DeviceIdType.MESH


def rounded(value):
    return float(np.asarray(value, ml_dtypes.bfloat16))


HEADS = tuple(rounded(c) for c in COEFS)
RESTS = tuple(rounded(c - h) for c, h in zip(COEFS, HEADS))


def kernel(
    sizes,
    now_ref,
    before_ref,
    speed_ref,
    born_ref,
    pml_x_ref,
    pml_y_ref,
    src_x_ref,
    src_y_ref,
    amp_ref,
    rec_x_ref,
    rec_y_ref,
    res_ref,
    out_ref,
    sums_ref,
    curv_ref,
    field0,
    field1,
    prev,
    speed,
    born,
    terms,
    sib,
    lap,
    band,
    corner,
    direct,
    x_send,
    x_recv,
    y_send,
    y_recv,
    packed,
    edge,
    sides,
    planes,
    curv_sib,
    curv_y,
    curv_x,
    curv_z,
    far_x,
    far_y,
    at_x,
    at_y,
    pulse,
    recs_x,
    recs_y,
    weigh,
    in_sems,
    small_sems,
    x_sems,
    y_sems,
    sib_sems,
    rs_sems,
    ag_sems,
    agsib_sems,
    cs_sems,
    cy_sems,
    cx_sems,
    cz_sems,
    relay,
):
    shots, n_x, n_y = sizes
    n_z = shots // 2
    per = LEVELS // n_z
    shot = lax.axis_index("shot")
    core = lax.rem(shot, 2)
    z = shot // 2
    gx = lax.axis_index("gx")
    gy = lax.axis_index("gy")

    def z_id(k):
        return {"shot": lax.rem(z + k + 2 * n_z, n_z) * 2 + core}

    def x_id(k):
        return {"gx": lax.rem(gx + k + n_x, n_x)}

    def y_id(k):
        return {"gy": lax.rem(gy + k + n_y, n_y)}

    sib_id = {"shot": 2 * z + 1 - core}

    def remote(src, dst, send, recv, who):
        return pltpu.make_async_remote_copy(
            src_ref=src, dst_ref=dst, send_sem=send, recv_sem=recv, device_id=who, device_id_type=MESH
        )

    loads = [
        pltpu.make_async_copy(
            now_ref.at[0, pl.ds(2 * pair, 2)],
            field0.at[pl.ds(2 * pair, 2), :, pl.ds(8, ROWS), :],
            in_sems.at[pair],
        )
        for pair in range(2)
    ] + [
        pltpu.make_async_copy(before_ref.at[0], prev, in_sems.at[2]),
        pltpu.make_async_copy(speed_ref, speed, in_sems.at[3]),
        pltpu.make_async_copy(born_ref, born, in_sems.at[4]),
    ]
    small = [
        pltpu.make_async_copy(source, target, small_sems.at[i])
        for i, (source, target) in enumerate(
            [
                (pml_x_ref, far_x),
                (pml_y_ref, far_y),
                (src_x_ref, at_x),
                (src_y_ref, at_y),
                (amp_ref, pulse),
                (rec_x_ref, recs_x),
                (rec_y_ref, recs_y),
                (res_ref, weigh),
            ]
        )
    ]
    barrier = pltpu.get_barrier_semaphore()
    neighbours = [z_id(1), z_id(-1), x_id(1), x_id(-1), y_id(1), y_id(-1)]
    partners = [sib_id] + neighbours
    for who in partners:
        pl.semaphore_signal(barrier, inc=1, device_id=who, device_id_type=MESH)

    def tell(turn):
        for who in neighbours:
            pl.semaphore_signal(relay.at[turn], inc=1, device_id=who, device_id_type=MESH)

    def hear(turn):
        pl.semaphore_wait(relay.at[turn], len(neighbours))

    for load in loads[:2] + small + loads[2:]:
        load.start()

    whole_x = n_x * ROWS
    whole_y = n_y * COLS

    def build_planes():
        for load in small:
            load.wait()
        row0 = gx * ROWS
        col0 = gy * COLS
        row = row0 + lax.broadcasted_iota(jnp.int32, (ROWS, COLS), 0)
        col = col0 + lax.broadcasted_iota(jnp.int32, (ROWS, COLS), 1)

        def layer(place, length, far):
            value = jnp.maximum(jnp.maximum(PML_W - place, far - (length - 1 - place)), 0)
            return value.astype(jnp.float32) / PML_W

        layer_x = layer(row, whole_x, far_x[whole_x - 1])
        layer_y = layer(col, whole_y, far_y[whole_y - 1])
        damp = layer_x * layer_x + layer_y * layer_y
        inverse = 1.0 / (1.0 + damp)
        planes[0] = inverse
        planes[1] = (1.0 - damp) * inverse
        at_source = (row == at_x[0]) & (col == at_y[0])
        planes[2] = jnp.where(at_source, pulse[0, 0], 0.0)
        planes[3] = jnp.where(at_source, pulse[0, 1], 0.0)
        count_rec = recs_x.shape[1]
        hot_x = recs_x[...] == row0 + lax.broadcasted_iota(jnp.int32, (ROWS, count_rec), 0)
        hot_y = recs_y[...] == col0 + lax.broadcasted_iota(jnp.int32, (COLS, count_rec), 0)
        weights = [jnp.ones((1, count_rec), jnp.float32)]
        for turn in range(2):
            rest = weigh[0, turn : turn + 1, :]
            for _ in range(3):
                head = rest.astype(jnp.bfloat16).astype(jnp.float32)
                weights.append(head)
                rest = rest - head
        left = jnp.concatenate([jnp.where(hot_x, w, 0.0).astype(jnp.bfloat16) for w in weights], axis=0)
        right = jnp.where(hot_y, 1.0, 0.0).astype(jnp.bfloat16)
        hits = lax.dot_general(
            left, right, (((1,), (1,)), ((), ())), preferred_element_type=jnp.float32
        )
        parts = [hits[i * ROWS : (i + 1) * ROWS] for i in range(7)]
        planes[4] = parts[1] + parts[2] + parts[3]
        planes[5] = parts[4] + parts[5] + parts[6]
        planes[6] = parts[0]

    lane = lax.broadcasted_iota(jnp.int32, (8, COLS), 1)
    group = ((lane + 4) & (COLS - 1)) // 8

    def build_weights():
        shape = (2 * COLS, 2 * COLS)
        row = lax.broadcasted_iota(jnp.int32, shape, 0)
        col = lax.broadcasted_iota(jnp.int32, shape, 1)
        second = col >= COLS
        row = row & (COLS - 1)
        col = col & (COLS - 1)
        away = jnp.abs(row - col)
        ahead = (col - row) & (COLS - 1)
        ahead = jnp.where((row & 4) != 0, ahead, COLS - ahead)
        crosses = (row & 4) != (col & 4)
        near = jnp.zeros(shape, jnp.float32)
        far = jnp.zeros(shape, jnp.float32)
        for k in range(1, 5):
            value = jnp.where(second, RESTS[k], HEADS[k])
            near = jnp.where(away == k, value, near)
            far = jnp.where((ahead == k) & crosses, value, far)
        band[...] = near.astype(jnp.bfloat16)
        corner[...] = far.astype(jnp.bfloat16)

    def times(values, weights):
        head = values.astype(jnp.bfloat16)
        rest = (values - head.astype(jnp.float32)).astype(jnp.bfloat16)
        both = jnp.dot(
            jnp.concatenate([head, rest], axis=1), weights[...], preferred_element_type=jnp.float32
        )
        return both[:, :COLS] + both[:, COLS:]

    def block(b):
        return pl.ds(pl.multiple_of(b * 8, 8), 8)

    def inner(b, shift=0):
        return pl.ds(pl.multiple_of(b * 8, 8) + (8 + shift), 8)

    def pack_x(field, turn, pair):
        for i in range(16):
            f, lev = 2 * pair + i // LEVELS, i % LEVELS
            x_send[turn, pair, 0, i] = field[f, lev, 8:12, :]
            x_send[turn, pair, 1, i] = field[f, lev, ROWS + 4 : ROWS + 8, :]

    def borders(values):
        total = values[0]
        for i in range(1, 16):
            total = jnp.where(group == i, pltpu.roll(values[i], 8 * i, 1), total)
        return total

    def pack_y(field, pair):
        def body(b, carry):
            values = [field[2 * pair + i // LEVELS, i % LEVELS, inner(b), :] for i in range(16)]
            packed[pair, block(b), :] = borders(values)
            return carry

        lax.fori_loop(0, BLOCKS, body, 0)

    half_rows = ROWS // 2
    is_tail = (lax.broadcasted_iota(jnp.int32, (half_rows, COLS), 1) & 4) != 0

    def fold_y(turn, pair):
        first = packed[pair, 0:half_rows, :]
        second = packed[pair, half_rows:ROWS, :]
        y_send[turn, pair, 0] = jnp.where(is_tail, first, pltpu.roll(second, 4, 1))
        y_send[turn, pair, 1] = jnp.where(is_tail, pltpu.roll(second, COLS - 4, 1), first)

    def halos(buffer_out, buffer_in, sems, turn, pair, ident, ways):
        copies = [
            remote(
                buffer_out.at[turn, pair, way],
                buffer_in.at[turn, pair, way],
                sems.at[0, turn, pair, way],
                sems.at[1, turn, pair, way],
                ident(ways[way]),
            )
            for way in range(2)
        ]
        for copy in copies:
            copy.start()
        return copies

    def send_x(turn, pair):
        return halos(x_send, x_recv, x_sems, turn, pair, x_id, (-1, 1))

    def send_y(turn, pair):
        fold_y(turn, pair)
        return halos(y_send, y_recv, y_sems, turn, pair, y_id, (1, -1))

    def inside(field, pair):
        def along_y(f, carry):
            values = field[f, :, 8 : 8 + ROWS, :].reshape(LEVELS * ROWS, COLS)
            lap[f] = times(values, band).reshape(LEVELS, ROWS, COLS)
            return carry

        lax.fori_loop(2 * pair, 2 * pair + 2, along_y, 0)

        def along_xz(b, carry):
            for f in (2 * pair, 2 * pair + 1):
                centre = [field[f, lev, inner(b), :] for lev in range(LEVELS)]
                for lev in range(LEVELS):
                    total = lap[f, lev, block(b), :] + (3.0 * COEFS[0]) * centre[lev]
                    for k in range(1, 5):
                        near = field[f, lev, inner(b, k), :] + field[f, lev, inner(b, -k), :]
                        if lev + k < LEVELS:
                            near += centre[lev + k]
                        if lev - k >= 0:
                            near += centre[lev - k]
                        total += COEFS[k] * near
                    lap[f, lev, block(b), :] = total
            return carry

        lax.fori_loop(0, BLOCKS, along_xz, 0)

    def unpack_y(turn, pair):
        tails = jnp.where(gy == 0, 0.0, y_recv[turn, pair, 0])
        heads = jnp.where(gy == n_y - 1, 0.0, y_recv[turn, pair, 1])
        first = jnp.where(is_tail, tails, heads)
        second = jnp.where(is_tail, pltpu.roll(tails, COLS - 4, 1), pltpu.roll(heads, 4, 1))
        sides[pair] = times(jnp.concatenate([first, second], axis=0), corner)

    def unpack_x(turn, pair):
        def body(f, carry):
            for lev in range(LEVELS):
                i = f * LEVELS + lev
                mine = (f - 2 * pair) * LEVELS + lev
                edge[0, i, 4:8, :] = jnp.where(gx == 0, 0.0, x_recv[turn, pair, 1, mine])
                edge[1, i, 8:12, :] = jnp.where(gx == n_x - 1, 0.0, x_recv[turn, pair, 0, mine])
            for lev in range(LEVELS):
                i = f * LEVELS + lev
                top = lap[f, lev, 0:8, :]
                bottom = lap[f, lev, ROWS - 8 : ROWS, :]
                for k in range(1, 5):
                    top += COEFS[k] * edge[0, i, 8 - k : 16 - k, :]
                    bottom += COEFS[k] * edge[1, i, k : k + 8, :]
                lap[f, lev, 0:8, :] = top
                lap[f, lev, ROWS - 8 : ROWS, :] = bottom
            return carry

        lax.fori_loop(2 * pair, 2 * pair + 2, body, 0)

    outer = (lane < 4) | (lane >= COLS - 4)

    def laplace(f, b):
        side = sides[f // 2, block(b), :]
        results = []
        for lev in range(LEVELS):
            at = (8 * (f % 2) + lev) * 8
            turned = pltpu.roll(side, COLS - at, 1) if at else side
            results.append(lap[f, lev, block(b), :] + jnp.where(outer, turned, 0.0))
        return results

    def old(turn, f, lev, b):
        return prev[f, lev, block(b), :] if turn == 0 else field0[f, lev, inner(b), :]

    def finish(turn, pair, b, fresh):
        for i in range(16):
            f, lev = 2 * pair + i // LEVELS, i % LEVELS
            if turn == 0:
                field1[f, lev, inner(b), :] = fresh[i]
            else:
                out_ref[0, f, lev, block(b), :] = fresh[i]
        if turn == 0:
            packed[pair, block(b), :] = borders(fresh)

    def incident(turn, field, first, last, curv):
        def body(b, curv):
            u = [field[0, lev, inner(b), :] for lev in range(LEVELS)]
            du = [field[1, lev, inner(b), :] for lev in range(LEVELS)]
            lap_u = laplace(0, b)
            lap_du = laplace(1, b)
            fresh = [None] * 16
            inv = planes[0, block(b), :]
            fade = planes[1, block(b), :]
            for lev in range(LEVELS):
                lam = field[2, lev, inner(b), :]
                dlam = field[3, lev, inner(b), :]
                grad = lam * lap_u[lev]
                hess = dlam * lap_u[lev] + lam * lap_du[lev]
                if turn == 1:
                    grad += terms[0, lev, block(b), :]
                    hess += terms[1, lev, block(b), :]
                terms[0, lev, block(b), :] = grad
                terms[1, lev, block(b), :] = hess
                direction = born[lev, block(b), :]
                if turn == 1:
                    curv += direction * hess
                pace = speed[lev, block(b), :]
                new_u = 2.0 * u[lev] + pace * lap_u[lev]
                if lev == 1:
                    new_u += planes[2 + turn, block(b), :]
                new_du = 2.0 * du[lev] + pace * lap_du[lev] + direction * lap_u[lev]
                fresh[lev] = new_u * inv - fade * old(turn, 0, lev, b)
                fresh[LEVELS + lev] = new_du * inv - fade * old(turn, 1, lev, b)
            finish(turn, 0, b, fresh)
            return curv

        return lax.fori_loop(first, last, body, curv)

    def adjoint(turn, field):
        def body(b, carry):
            lam = [field[2, lev, inner(b), :] for lev in range(LEVELS)]
            dlam = [field[3, lev, inner(b), :] for lev in range(LEVELS)]
            lap_lam = laplace(2, b)
            lap_dlam = laplace(3, b)
            fresh = [None] * 16
            inv = planes[0, block(b), :]
            fade = planes[1, block(b), :]
            for lev in range(LEVELS):
                pace = speed[lev, block(b), :]
                new_lam = 2.0 * lam[lev] + pace * lap_lam[lev]
                new_dlam = 2.0 * dlam[lev] + pace * lap_dlam[lev] + born[lev, block(b), :] * lap_lam[lev]
                if lev == 1:
                    new_lam += planes[4 + turn, block(b), :]
                    new_dlam += planes[6, block(b), :] * field[1, lev, inner(b), :]
                fresh[lev] = new_lam * inv - fade * old(turn, 2, lev, b)
                fresh[LEVELS + lev] = new_dlam * inv - fade * old(turn, 3, lev, b)
            finish(turn, 1, b, fresh)
            return carry

        lax.fori_loop(0, BLOCKS, body, 0)

    for field in (field0, field1):
        for f in range(4):
            for lev in range(LEVELS):
                field[f, lev, 0:8, :] = jnp.zeros((8, COLS), jnp.float32)
                field[f, lev, ROWS + 8 : ROWS + 16, :] = jnp.zeros((8, COLS), jnp.float32)
    for i in range(32):
        edge[0, i, 0:8, :] = jnp.zeros((8, COLS), jnp.float32)
        edge[0, i, 8:16, :] = jnp.zeros((8, COLS), jnp.float32)
        edge[1, i, 0:8, :] = jnp.zeros((8, COLS), jnp.float32)
        edge[1, i, 8:16, :] = jnp.zeros((8, COLS), jnp.float32)
    x_copies = {}
    y_copies = {}
    for pair in range(2):
        loads[pair].wait()
        pack_x(field0, 0, pair)
        if pair == 0:
            pl.semaphore_wait(barrier, len(partners))
        x_copies[0, pair] = send_x(0, pair)
        pack_y(field0, pair)
        y_copies[0, pair] = send_y(0, pair)
    tell(0)
    build_weights()
    build_planes()
    inside(field0, 0)
    inside(field0, 1)
    hear(0)
    tell(1)
    for load in loads[2:]:
        load.wait()

    def take(turn, pair):
        for copy in y_copies[turn, pair]:
            copy.wait_recv()
        unpack_y(turn, pair)
        for copy in x_copies[turn, pair]:
            copy.wait_recv()
        unpack_x(turn, pair)

    take(0, 0)
    nothing = jnp.zeros((8, COLS), jnp.float32)
    incident(0, field0, 0, BLOCKS, nothing)
    pack_x(field1, 1, 0)
    x_copies[1, 0] = send_x(1, 0)
    y_copies[1, 0] = send_y(1, 0)
    take(0, 1)
    adjoint(0, field0)
    pack_x(field1, 1, 1)
    x_copies[1, 1] = send_x(1, 1)
    y_copies[1, 1] = send_y(1, 1)

    hear(1)
    tell(2)
    inside(field1, 0)
    inside(field1, 1)
    take(1, 0)

    halves = (pl.ds(0, ROWS // 2), pl.ds(ROWS // 2, ROWS // 2))
    swaps = []
    curv = nothing
    for part in range(2):
        curv = incident(1, field1, part * (BLOCKS // 2), (part + 1) * (BLOCKS // 2), curv)
        swap = remote(
            terms.at[1 - core, :, halves[part], :],
            sib.at[:, halves[part], :],
            sib_sems.at[0, part],
            sib_sems.at[1, part],
            sib_id,
        )
        swap.start()
        swaps.append(swap)
    curv_sib[core] = curv
    curv_swap = remote(curv_sib.at[core], curv_sib.at[core], cs_sems.at[0], cs_sems.at[1], sib_id)
    curv_swap.start()
    take(1, 1)
    hear(2)

    def spread(buffer, place, value, sems, ident, count):
        buffer[place] = value
        sent = [
            remote(buffer.at[place], buffer.at[place], sems.at[0, k - 1], sems.at[1, k - 1], ident(k))
            for k in range(1, count)
        ]
        for copy in sent:
            copy.start()
        return sent

    def gather(sent, buffer, count):
        for copy in sent:
            copy.wait()
        total = buffer[0]
        for k in range(1, count):
            total = total + buffer[k]
        return total

    def owner(k):
        return pl.ds(lax.rem(z + k + 2 * n_z, n_z) * per, per)

    order = sorted(range(1, n_z), key=lambda k: -min(k, n_z - k))
    shares = {}
    for part in range(2):
        rows = halves[part]
        swaps[part].wait_recv()
        for k in order:
            level = owner(k)
            terms[core, level, rows, :] = terms[core, level, rows, :] + sib[level, rows, :]
            shares[part, k] = remote(
                terms.at[core, level, rows, :],
                direct.at[part, k - 1],
                rs_sems.at[0, part, k - 1],
                rs_sems.at[1, part, k - 1],
                z_id(k),
            )
            shares[part, k].start()
        if part == 0:
            curv_swap.wait()
            curv = curv_sib[0] + curv_sib[1]
            sent_y = spread(curv_x, gx, curv, cx_sems, x_id, n_x)
    adjoint(1, field1)

    def pass_on(level, rows, sems, part, k, who):
        copy = remote(
            sums_ref.at[core, level, rows, :],
            sums_ref.at[core, level, rows, :],
            sems.at[0, part, k],
            sems.at[1, part, k],
            who,
        )
        copy.start()
        return copy

    spreads = {}
    across = []
    for part in range(2):
        rows = halves[part]
        total = terms[core, owner(0), rows, :] + sib[owner(0), rows, :]
        for k in reversed(order):
            shares[part, k].wait_recv()
            total = total + direct[part, k - 1]
        sums_ref[core, owner(0), rows, :] = total * (1.0 / shots)
        for k in order:
            spreads[part, k] = pass_on(owner(0), rows, ag_sems, part, k - 1, z_id(k))
        across.append(pass_on(owner(0), rows, agsib_sems, part, 0, sib_id))
        if part == 0:
            curv = gather(sent_y, curv_x, n_x)
            sent_x = spread(curv_y, gy, curv, cy_sems, y_id, n_y)
    curv = gather(sent_x, curv_y, n_y)
    sent_z = spread(curv_z, z, curv, cz_sems, z_id, n_z)
    for part in range(2):
        for k in reversed(order):
            spreads[part, k].wait_recv()
            across.append(pass_on(owner(-k), halves[part], agsib_sems, part, k, sib_id))
    curv = gather(sent_z, curv_z, n_z)
    cells = LEVELS * whole_x * whole_y
    curv_ref[...] = jnp.sum(curv, keepdims=True) * (1.0 / (shots * math.sqrt(cells)))
    for copies in list(x_copies.values()) + list(y_copies.values()):
        for copy in copies:
            copy.wait_send()
    for copy in swaps + list(shares.values()) + list(spreads.values()):
        copy.wait_send()
    for copy in across:
        copy.wait()


def deliver(fields_ref, sums_ref, curv_ref, out_ref, grad_ref, hess_ref, total_ref, sems):
    copies = [
        pltpu.make_async_copy(source, target, sems.at[i])
        for i, (source, target) in enumerate(
            [
                (fields_ref, out_ref),
                (sums_ref.at[0], grad_ref),
                (sums_ref.at[1], hess_ref),
                (curv_ref, total_ref),
            ]
        )
    ]
    for copy in copies:
        copy.start()
    for copy in copies:
        copy.wait()


def local(sizes, *args):
    shots, n_x, n_y = sizes
    n_z = shots // 2
    per = LEVELS // n_z
    any_space = pl.BlockSpec(memory_space=pl.ANY)
    hbm = pl.BlockSpec(memory_space=pltpu.HBM)
    vmem = pl.BlockSpec(memory_space=pltpu.VMEM)
    f32 = jnp.float32
    dma = pltpu.SemaphoreType.DMA
    tile = (8, COLS)
    fields, sums, curv = pl.pallas_call(
        functools.partial(kernel, sizes),
        out_shape=(
            pltpu.VMEM((1, 4, LEVELS, ROWS, COLS), f32),
            pltpu.VMEM((2, LEVELS, ROWS, COLS), f32),
            pltpu.VMEM((1, 1), f32),
        ),
        in_specs=[any_space] * 12,
        out_specs=(vmem,) * 3,
        scratch_shapes=[
            pltpu.VMEM((4, LEVELS, ROWS + 16, COLS), f32),
            pltpu.VMEM((4, LEVELS, ROWS + 16, COLS), f32),
            pltpu.VMEM((4, LEVELS, ROWS, COLS), f32),
            pltpu.VMEM((LEVELS, ROWS, COLS), f32),
            pltpu.VMEM((LEVELS, ROWS, COLS), f32),
            pltpu.VMEM((2, LEVELS, ROWS, COLS), f32),
            pltpu.VMEM((LEVELS, ROWS, COLS), f32),
            pltpu.VMEM((4, LEVELS, ROWS, COLS), f32),
            pltpu.VMEM((2 * COLS, 2 * COLS), jnp.bfloat16),
            pltpu.VMEM((2 * COLS, 2 * COLS), jnp.bfloat16),
            pltpu.VMEM((2, n_z - 1, per, ROWS // 2, COLS), f32),
            pltpu.VMEM((2, 2, 2, 16, 4, COLS), f32),
            pltpu.VMEM((2, 2, 2, 16, 4, COLS), f32),
            pltpu.VMEM((2, 2, 2, ROWS // 2, COLS), f32),
            pltpu.VMEM((2, 2, 2, ROWS // 2, COLS), f32),
            pltpu.VMEM((2, ROWS, COLS), f32),
            pltpu.VMEM((2, 32, 16, COLS), f32),
            pltpu.VMEM((2, ROWS, COLS), f32),
            pltpu.VMEM((7, ROWS, COLS), f32),
            pltpu.VMEM((2,) + tile, f32),
            pltpu.VMEM((n_y,) + tile, f32),
            pltpu.VMEM((n_x,) + tile, f32),
            pltpu.VMEM((n_z,) + tile, f32),
            pltpu.SMEM(args[4].shape, jnp.int32),
            pltpu.SMEM(args[5].shape, jnp.int32),
            pltpu.SMEM((1,), jnp.int32),
            pltpu.SMEM((1,), jnp.int32),
            pltpu.SMEM(args[8].shape, f32),
            pltpu.VMEM(args[9].shape, jnp.int32),
            pltpu.VMEM(args[10].shape, jnp.int32),
            pltpu.VMEM(args[11].shape, f32),
            dma((5,)),
            dma((8,)),
            dma((2, 2, 2, 2)),
            dma((2, 2, 2, 2)),
            dma((2, 2)),
            dma((2, 2, n_z - 1)),
            dma((2, 2, n_z - 1)),
            dma((2, 2, n_z)),
            dma((2,)),
            dma((2, n_y - 1)),
            dma((2, n_x - 1)),
            dma((2, n_z - 1)),
            pltpu.SemaphoreType.REGULAR((3,)),
        ],
        compiler_params=pltpu.CompilerParams(
            collective_id=0, has_side_effects=True, vmem_limit_bytes=32 * 1024 * 1024
        ),
    )(*[arg if arg.size == 1 else pltpu.with_memory_space_constraint(arg, pltpu.HBM) for arg in args])
    sums_shape = jax.ShapeDtypeStruct((LEVELS, ROWS, COLS), f32)
    fields, grad, hess, curv = pl.pallas_call(
        deliver,
        out_shape=(jax.ShapeDtypeStruct(fields.shape, f32), sums_shape, sums_shape, jax.ShapeDtypeStruct((1, 1), f32)),
        in_specs=[any_space] * 3,
        out_specs=(hbm,) * 4,
        scratch_shapes=[dma((4,))],
    )(*[pltpu.with_memory_space_constraint(value, pltpu.VMEM) for value in (fields, sums, curv)])
    return fields, grad, hess, curv[0, 0]


def solution(mesh):
    sizes = (mesh.shape["shot"], mesh.shape["gx"], mesh.shape["gy"])
    placed = (
        P("shot", None, None, "gx", "gy"),
        P("shot", None, None, "gx", "gy"),
        P(None, "gx", "gy"),
        P(None, "gx", "gy"),
        P(),
        P(),
        P("shot"),
        P("shot"),
        P("shot", None),
        P("shot", None),
        P("shot", None),
        P("shot", None, None),
    )
    return jax.shard_map(
        functools.partial(local, sizes),
        mesh=mesh,
        in_specs=placed,
        out_specs=(
            P("shot", None, None, "gx", "gy"),
            P(None, "gx", "gy"),
            P(None, "gx", "gy"),
            P(),
        ),
        check_vma=False,
    )
```

```python
import functools
import math

import jax
import jax.numpy as jnp
import ml_dtypes
import numpy as np
from jax import lax
from jax.experimental import pallas as pl
from jax.experimental.pallas import tpu as pltpu
from jax.sharding import PartitionSpec as P

PML_W = 16
COEFS = (-205.0 / 72.0, 8.0 / 5.0, -1.0 / 5.0, 8.0 / 315.0, -1.0 / 560.0)
LEVELS = 8
ROWS = 64
COLS = 128
BLOCKS = ROWS // 8
MESH = pl.DeviceIdType.MESH


def rounded(value):
    return float(np.asarray(value, ml_dtypes.bfloat16))


HEADS = tuple(rounded(c) for c in COEFS)
RESTS = tuple(rounded(c - h) for c, h in zip(COEFS, HEADS))


def kernel(
    sizes,
    now_ref,
    before_ref,
    speed_ref,
    born_ref,
    pml_x_ref,
    pml_y_ref,
    src_x_ref,
    src_y_ref,
    amp_ref,
    rec_x_ref,
    rec_y_ref,
    res_ref,
    out_ref,
    sums_ref,
    curv_ref,
    field0,
    field1,
    prev,
    speed,
    born,
    terms,
    sib,
    lap,
    band,
    corner,
    direct,
    x_send,
    x_recv,
    y_send,
    y_recv,
    packed,
    edge,
    sides,
    planes,
    curv_sib,
    curv_y,
    curv_x,
    curv_z,
    far_x,
    far_y,
    at_x,
    at_y,
    pulse,
    recs_x,
    recs_y,
    weigh,
    in_sems,
    small_sems,
    x_sems,
    y_sems,
    sib_sems,
    rs_sems,
    ag_sems,
    agsib_sems,
    cs_sems,
    cy_sems,
    cx_sems,
    cz_sems,
    relay,
):
    shots, n_x, n_y = sizes
    n_z = shots // 2
    per = LEVELS // n_z
    shot = lax.axis_index("shot")
    core = lax.rem(shot, 2)
    z = shot // 2
    gx = lax.axis_index("gx")
    gy = lax.axis_index("gy")

    def z_id(k):
        return {"shot": lax.rem(z + k + 2 * n_z, n_z) * 2 + core}

    def x_id(k):
        return {"gx": lax.rem(gx + k + n_x, n_x)}

    def y_id(k):
        return {"gy": lax.rem(gy + k + n_y, n_y)}

    sib_id = {"shot": 2 * z + 1 - core}

    def remote(src, dst, send, recv, who):
        return pltpu.make_async_remote_copy(
            src_ref=src, dst_ref=dst, send_sem=send, recv_sem=recv, device_id=who, device_id_type=MESH
        )

    loads = [
        pltpu.make_async_copy(
            now_ref.at[0, pl.ds(2 * pair, 2)],
            field0.at[pl.ds(2 * pair, 2), :, pl.ds(8, ROWS), :],
            in_sems.at[pair],
        )
        for pair in range(2)
    ] + [
        pltpu.make_async_copy(before_ref.at[0], prev, in_sems.at[2]),
        pltpu.make_async_copy(speed_ref, speed, in_sems.at[3]),
        pltpu.make_async_copy(born_ref, born, in_sems.at[4]),
    ]
    small = [
        pltpu.make_async_copy(source, target, small_sems.at[i])
        for i, (source, target) in enumerate(
            [
                (pml_x_ref, far_x),
                (pml_y_ref, far_y),
                (src_x_ref, at_x),
                (src_y_ref, at_y),
                (amp_ref, pulse),
                (rec_x_ref, recs_x),
                (rec_y_ref, recs_y),
                (res_ref, weigh),
            ]
        )
    ]
    barrier = pltpu.get_barrier_semaphore()
    neighbours = [z_id(1), z_id(-1), x_id(1), x_id(-1), y_id(1), y_id(-1)]
    partners = [sib_id] + neighbours
    for who in partners:
        pl.semaphore_signal(barrier, inc=1, device_id=who, device_id_type=MESH)

    def tell(turn):
        for who in neighbours:
            pl.semaphore_signal(relay.at[turn], inc=1, device_id=who, device_id_type=MESH)

    def hear(turn):
        pl.semaphore_wait(relay.at[turn], len(neighbours))

    for load in loads[:2] + small + loads[2:]:
        load.start()

    whole_x = n_x * ROWS
    whole_y = n_y * COLS

    def build_planes():
        for load in small:
            load.wait()
        row0 = gx * ROWS
        col0 = gy * COLS
        row = row0 + lax.broadcasted_iota(jnp.int32, (ROWS, COLS), 0)
        col = col0 + lax.broadcasted_iota(jnp.int32, (ROWS, COLS), 1)

        def layer(place, length, far):
            value = jnp.maximum(jnp.maximum(PML_W - place, far - (length - 1 - place)), 0)
            return value.astype(jnp.float32) / PML_W

        layer_x = layer(row, whole_x, far_x[whole_x - 1])
        layer_y = layer(col, whole_y, far_y[whole_y - 1])
        damp = layer_x * layer_x + layer_y * layer_y
        inverse = 1.0 / (1.0 + damp)
        planes[0] = inverse
        planes[1] = (1.0 - damp) * inverse
        at_source = (row == at_x[0]) & (col == at_y[0])
        planes[2] = jnp.where(at_source, pulse[0, 0], 0.0)
        planes[3] = jnp.where(at_source, pulse[0, 1], 0.0)
        count_rec = recs_x.shape[1]
        hot_x = recs_x[...] == row0 + lax.broadcasted_iota(jnp.int32, (ROWS, count_rec), 0)
        hot_y = recs_y[...] == col0 + lax.broadcasted_iota(jnp.int32, (COLS, count_rec), 0)
        weights = [jnp.ones((1, count_rec), jnp.float32)]
        for turn in range(2):
            rest = weigh[0, turn : turn + 1, :]
            for _ in range(3):
                head = rest.astype(jnp.bfloat16).astype(jnp.float32)
                weights.append(head)
                rest = rest - head
        left = jnp.concatenate([jnp.where(hot_x, w, 0.0).astype(jnp.bfloat16) for w in weights], axis=0)
        right = jnp.where(hot_y, 1.0, 0.0).astype(jnp.bfloat16)
        hits = lax.dot_general(
            left, right, (((1,), (1,)), ((), ())), preferred_element_type=jnp.float32
        )
        parts = [hits[i * ROWS : (i + 1) * ROWS] for i in range(7)]
        planes[4] = parts[1] + parts[2] + parts[3]
        planes[5] = parts[4] + parts[5] + parts[6]
        planes[6] = parts[0]

    lane = lax.broadcasted_iota(jnp.int32, (8, COLS), 1)
    group = ((lane + 4) & (COLS - 1)) // 8

    def build_weights():
        shape = (2 * COLS, 2 * COLS)
        row = lax.broadcasted_iota(jnp.int32, shape, 0)
        col = lax.broadcasted_iota(jnp.int32, shape, 1)
        second = col >= COLS
        row = row & (COLS - 1)
        col = col & (COLS - 1)
        away = jnp.abs(row - col)
        ahead = (col - row) & (COLS - 1)
        ahead = jnp.where((row & 4) != 0, ahead, COLS - ahead)
        crosses = (row & 4) != (col & 4)
        near = jnp.zeros(shape, jnp.float32)
        far = jnp.zeros(shape, jnp.float32)
        for k in range(1, 5):
            value = jnp.where(second, RESTS[k], HEADS[k])
            near = jnp.where(away == k, value, near)
            far = jnp.where((ahead == k) & crosses, value, far)
        band[...] = near.astype(jnp.bfloat16)
        corner[...] = far.astype(jnp.bfloat16)

    def times(values, weights):
        head = values.astype(jnp.bfloat16)
        rest = (values - head.astype(jnp.float32)).astype(jnp.bfloat16)
        both = jnp.dot(
            jnp.concatenate([head, rest], axis=1), weights[...], preferred_element_type=jnp.float32
        )
        return both[:, :COLS] + both[:, COLS:]

    def block(b):
        return pl.ds(pl.multiple_of(b * 8, 8), 8)

    def inner(b, shift=0):
        return pl.ds(pl.multiple_of(b * 8, 8) + (8 + shift), 8)

    def pack_x(field, turn, pair):
        for i in range(16):
            f, lev = 2 * pair + i // LEVELS, i % LEVELS
            x_send[turn, pair, 0, i] = field[f, lev, 8:12, :]
            x_send[turn, pair, 1, i] = field[f, lev, ROWS + 4 : ROWS + 8, :]

    def borders(values):
        total = values[0]
        for i in range(1, 16):
            total = jnp.where(group == i, pltpu.roll(values[i], 8 * i, 1), total)
        return total

    def pack_y(field, pair):
        def body(b, carry):
            values = [field[2 * pair + i // LEVELS, i % LEVELS, inner(b), :] for i in range(16)]
            packed[pair, block(b), :] = borders(values)
            return carry

        lax.fori_loop(0, BLOCKS, body, 0)

    half_rows = ROWS // 2
    is_tail = (lax.broadcasted_iota(jnp.int32, (half_rows, COLS), 1) & 4) != 0

    def fold_y(turn, pair):
        first = packed[pair, 0:half_rows, :]
        second = packed[pair, half_rows:ROWS, :]
        y_send[turn, pair, 0] = jnp.where(is_tail, first, pltpu.roll(second, 4, 1))
        y_send[turn, pair, 1] = jnp.where(is_tail, pltpu.roll(second, COLS - 4, 1), first)

    def halos(buffer_out, buffer_in, sems, turn, pair, ident, ways):
        copies = [
            remote(
                buffer_out.at[turn, pair, way],
                buffer_in.at[turn, pair, way],
                sems.at[0, turn, pair, way],
                sems.at[1, turn, pair, way],
                ident(ways[way]),
            )
            for way in range(2)
        ]
        for copy in copies:
            copy.start()
        return copies

    def send_x(turn, pair):
        return halos(x_send, x_recv, x_sems, turn, pair, x_id, (-1, 1))

    def send_y(turn, pair):
        fold_y(turn, pair)
        return halos(y_send, y_recv, y_sems, turn, pair, y_id, (1, -1))

    def inside(field, pair):
        def along_y(f, carry):
            values = field[f, :, 8 : 8 + ROWS, :].reshape(LEVELS * ROWS, COLS)
            lap[f] = times(values, band).reshape(LEVELS, ROWS, COLS)
            return carry

        lax.fori_loop(2 * pair, 2 * pair + 2, along_y, 0)

        def along_xz(b, carry):
            for f in (2 * pair, 2 * pair + 1):
                centre = [field[f, lev, inner(b), :] for lev in range(LEVELS)]
                for lev in range(LEVELS):
                    total = lap[f, lev, block(b), :] + (3.0 * COEFS[0]) * centre[lev]
                    for k in range(1, 5):
                        near = field[f, lev, inner(b, k), :] + field[f, lev, inner(b, -k), :]
                        if lev + k < LEVELS:
                            near += centre[lev + k]
                        if lev - k >= 0:
                            near += centre[lev - k]
                        total += COEFS[k] * near
                    lap[f, lev, block(b), :] = total
            return carry

        lax.fori_loop(0, BLOCKS, along_xz, 0)

    def unpack_y(turn, pair):
        tails = jnp.where(gy == 0, 0.0, y_recv[turn, pair, 0])
        heads = jnp.where(gy == n_y - 1, 0.0, y_recv[turn, pair, 1])
        first = jnp.where(is_tail, tails, heads)
        second = jnp.where(is_tail, pltpu.roll(tails, COLS - 4, 1), pltpu.roll(heads, 4, 1))
        sides[pair] = times(jnp.concatenate([first, second], axis=0), corner)

    def unpack_x(turn, pair):
        def body(f, carry):
            for lev in range(LEVELS):
                i = f * LEVELS + lev
                mine = (f - 2 * pair) * LEVELS + lev
                edge[0, i, 4:8, :] = jnp.where(gx == 0, 0.0, x_recv[turn, pair, 1, mine])
                edge[1, i, 8:12, :] = jnp.where(gx == n_x - 1, 0.0, x_recv[turn, pair, 0, mine])
            for lev in range(LEVELS):
                i = f * LEVELS + lev
                top = lap[f, lev, 0:8, :]
                bottom = lap[f, lev, ROWS - 8 : ROWS, :]
                for k in range(1, 5):
                    top += COEFS[k] * edge[0, i, 8 - k : 16 - k, :]
                    bottom += COEFS[k] * edge[1, i, k : k + 8, :]
                lap[f, lev, 0:8, :] = top
                lap[f, lev, ROWS - 8 : ROWS, :] = bottom
            return carry

        lax.fori_loop(2 * pair, 2 * pair + 2, body, 0)

    outer = (lane < 4) | (lane >= COLS - 4)

    def laplace(f, b):
        side = sides[f // 2, block(b), :]
        results = []
        for lev in range(LEVELS):
            at = (8 * (f % 2) + lev) * 8
            turned = pltpu.roll(side, COLS - at, 1) if at else side
            results.append(lap[f, lev, block(b), :] + jnp.where(outer, turned, 0.0))
        return results

    def old(turn, f, lev, b):
        return prev[f, lev, block(b), :] if turn == 0 else field0[f, lev, inner(b), :]

    def finish(turn, pair, b, fresh):
        for i in range(16):
            f, lev = 2 * pair + i // LEVELS, i % LEVELS
            if turn == 0:
                field1[f, lev, inner(b), :] = fresh[i]
            else:
                out_ref[0, f, lev, block(b), :] = fresh[i]
        if turn == 0:
            packed[pair, block(b), :] = borders(fresh)

    def incident(turn, field, first, last, curv):
        def body(b, curv):
            u = [field[0, lev, inner(b), :] for lev in range(LEVELS)]
            du = [field[1, lev, inner(b), :] for lev in range(LEVELS)]
            lap_u = laplace(0, b)
            lap_du = laplace(1, b)
            fresh = [None] * 16
            inv = planes[0, block(b), :]
            fade = planes[1, block(b), :]
            for lev in range(LEVELS):
                lam = field[2, lev, inner(b), :]
                dlam = field[3, lev, inner(b), :]
                grad = lam * lap_u[lev]
                hess = dlam * lap_u[lev] + lam * lap_du[lev]
                if turn == 1:
                    grad += terms[0, lev, block(b), :]
                    hess += terms[1, lev, block(b), :]
                terms[0, lev, block(b), :] = grad
                terms[1, lev, block(b), :] = hess
                direction = born[lev, block(b), :]
                if turn == 1:
                    curv += direction * hess
                pace = speed[lev, block(b), :]
                new_u = 2.0 * u[lev] + pace * lap_u[lev]
                if lev == 1:
                    new_u += planes[2 + turn, block(b), :]
                new_du = 2.0 * du[lev] + pace * lap_du[lev] + direction * lap_u[lev]
                fresh[lev] = new_u * inv - fade * old(turn, 0, lev, b)
                fresh[LEVELS + lev] = new_du * inv - fade * old(turn, 1, lev, b)
            finish(turn, 0, b, fresh)
            return curv

        return lax.fori_loop(first, last, body, curv)

    def adjoint(turn, field):
        def body(b, carry):
            lam = [field[2, lev, inner(b), :] for lev in range(LEVELS)]
            dlam = [field[3, lev, inner(b), :] for lev in range(LEVELS)]
            lap_lam = laplace(2, b)
            lap_dlam = laplace(3, b)
            fresh = [None] * 16
            inv = planes[0, block(b), :]
            fade = planes[1, block(b), :]
            for lev in range(LEVELS):
                pace = speed[lev, block(b), :]
                new_lam = 2.0 * lam[lev] + pace * lap_lam[lev]
                new_dlam = 2.0 * dlam[lev] + pace * lap_dlam[lev] + born[lev, block(b), :] * lap_lam[lev]
                if lev == 1:
                    new_lam += planes[4 + turn, block(b), :]
                    new_dlam += planes[6, block(b), :] * field[1, lev, inner(b), :]
                fresh[lev] = new_lam * inv - fade * old(turn, 2, lev, b)
                fresh[LEVELS + lev] = new_dlam * inv - fade * old(turn, 3, lev, b)
            finish(turn, 1, b, fresh)
            return carry

        lax.fori_loop(0, BLOCKS, body, 0)

    for field in (field0, field1):
        for f in range(4):
            for lev in range(LEVELS):
                field[f, lev, 0:8, :] = jnp.zeros((8, COLS), jnp.float32)
                field[f, lev, ROWS + 8 : ROWS + 16, :] = jnp.zeros((8, COLS), jnp.float32)
    for i in range(32):
        edge[0, i, 0:8, :] = jnp.zeros((8, COLS), jnp.float32)
        edge[0, i, 8:16, :] = jnp.zeros((8, COLS), jnp.float32)
        edge[1, i, 0:8, :] = jnp.zeros((8, COLS), jnp.float32)
        edge[1, i, 8:16, :] = jnp.zeros((8, COLS), jnp.float32)
    x_copies = {}
    y_copies = {}
    for pair in range(2):
        loads[pair].wait()
        pack_x(field0, 0, pair)
        if pair == 0:
            pl.semaphore_wait(barrier, len(partners))
        x_copies[0, pair] = send_x(0, pair)
        pack_y(field0, pair)
        y_copies[0, pair] = send_y(0, pair)
    tell(0)
    build_weights()
    build_planes()
    inside(field0, 0)
    inside(field0, 1)
    hear(0)
    tell(1)
    for load in loads[2:]:
        load.wait()

    def take(turn, pair):
        for copy in y_copies[turn, pair]:
            copy.wait_recv()
        unpack_y(turn, pair)
        for copy in x_copies[turn, pair]:
            copy.wait_recv()
        unpack_x(turn, pair)

    take(0, 0)
    nothing = jnp.zeros((8, COLS), jnp.float32)
    incident(0, field0, 0, BLOCKS, nothing)
    pack_x(field1, 1, 0)
    x_copies[1, 0] = send_x(1, 0)
    y_copies[1, 0] = send_y(1, 0)
    take(0, 1)
    adjoint(0, field0)
    pack_x(field1, 1, 1)
    x_copies[1, 1] = send_x(1, 1)
    y_copies[1, 1] = send_y(1, 1)

    hear(1)
    tell(2)
    inside(field1, 0)
    take(1, 0)

    halves = (pl.ds(0, ROWS // 2), pl.ds(ROWS // 2, ROWS // 2))
    swaps = []
    curv = nothing
    for part in range(2):
        curv = incident(1, field1, part * (BLOCKS // 2), (part + 1) * (BLOCKS // 2), curv)
        swap = remote(
            terms.at[1 - core, :, halves[part], :],
            sib.at[:, halves[part], :],
            sib_sems.at[0, part],
            sib_sems.at[1, part],
            sib_id,
        )
        swap.start()
        swaps.append(swap)
    curv_sib[core] = curv
    curv_swap = remote(curv_sib.at[core], curv_sib.at[core], cs_sems.at[0], cs_sems.at[1], sib_id)
    curv_swap.start()
    hear(2)

    def spread(buffer, place, value, sems, ident, count):
        buffer[place] = value
        sent = [
            remote(buffer.at[place], buffer.at[place], sems.at[0, k - 1], sems.at[1, k - 1], ident(k))
            for k in range(1, count)
        ]
        for copy in sent:
            copy.start()
        return sent

    def gather(sent, buffer, count):
        for copy in sent:
            copy.wait()
        total = buffer[0]
        for k in range(1, count):
            total = total + buffer[k]
        return total

    def owner(k):
        return pl.ds(lax.rem(z + k + 2 * n_z, n_z) * per, per)

    order = sorted(range(1, n_z), key=lambda k: -min(k, n_z - k))
    shares = {}
    for part in range(2):
        rows = halves[part]
        swaps[part].wait_recv()
        for k in order:
            level = owner(k)
            terms[core, level, rows, :] = terms[core, level, rows, :] + sib[level, rows, :]
            shares[part, k] = remote(
                terms.at[core, level, rows, :],
                direct.at[part, k - 1],
                rs_sems.at[0, part, k - 1],
                rs_sems.at[1, part, k - 1],
                z_id(k),
            )
            shares[part, k].start()
        if part == 0:
            curv_swap.wait()
            curv = curv_sib[0] + curv_sib[1]
            sent_y = spread(curv_x, gx, curv, cx_sems, x_id, n_x)
    inside(field1, 1)
    take(1, 1)
    adjoint(1, field1)

    def pass_on(level, rows, sems, part, k, who):
        copy = remote(
            sums_ref.at[core, level, rows, :],
            sums_ref.at[core, level, rows, :],
            sems.at[0, part, k],
            sems.at[1, part, k],
            who,
        )
        copy.start()
        return copy

    spreads = {}
    across = []
    for part in range(2):
        rows = halves[part]
        total = terms[core, owner(0), rows, :] + sib[owner(0), rows, :]
        for k in reversed(order):
            shares[part, k].wait_recv()
            total = total + direct[part, k - 1]
        sums_ref[core, owner(0), rows, :] = total * (1.0 / shots)
        for k in order:
            spreads[part, k] = pass_on(owner(0), rows, ag_sems, part, k - 1, z_id(k))
        across.append(pass_on(owner(0), rows, agsib_sems, part, 0, sib_id))
        if part == 0:
            curv = gather(sent_y, curv_x, n_x)
            sent_x = spread(curv_y, gy, curv, cy_sems, y_id, n_y)
    curv = gather(sent_x, curv_y, n_y)
    sent_z = spread(curv_z, z, curv, cz_sems, z_id, n_z)
    for part in range(2):
        for k in reversed(order):
            spreads[part, k].wait_recv()
            across.append(pass_on(owner(-k), halves[part], agsib_sems, part, k, sib_id))
    curv = gather(sent_z, curv_z, n_z)
    cells = LEVELS * whole_x * whole_y
    curv_ref[...] = jnp.sum(curv, keepdims=True) * (1.0 / (shots * math.sqrt(cells)))
    for copies in list(x_copies.values()) + list(y_copies.values()):
        for copy in copies:
            copy.wait_send()
    for copy in swaps + list(shares.values()) + list(spreads.values()):
        copy.wait_send()
    for copy in across:
        copy.wait()


def deliver(fields_ref, sums_ref, curv_ref, out_ref, grad_ref, hess_ref, total_ref, sems):
    copies = [
        pltpu.make_async_copy(source, target, sems.at[i])
        for i, (source, target) in enumerate(
            [
                (fields_ref, out_ref),
                (sums_ref.at[0], grad_ref),
                (sums_ref.at[1], hess_ref),
                (curv_ref, total_ref),
            ]
        )
    ]
    for copy in copies:
        copy.start()
    for copy in copies:
        copy.wait()


def local(sizes, *args):
    shots, n_x, n_y = sizes
    n_z = shots // 2
    per = LEVELS // n_z
    any_space = pl.BlockSpec(memory_space=pl.ANY)
    hbm = pl.BlockSpec(memory_space=pltpu.HBM)
    vmem = pl.BlockSpec(memory_space=pltpu.VMEM)
    f32 = jnp.float32
    dma = pltpu.SemaphoreType.DMA
    tile = (8, COLS)
    fields, sums, curv = pl.pallas_call(
        functools.partial(kernel, sizes),
        out_shape=(
            pltpu.VMEM((1, 4, LEVELS, ROWS, COLS), f32),
            pltpu.VMEM((2, LEVELS, ROWS, COLS), f32),
            pltpu.VMEM((1, 1), f32),
        ),
        in_specs=[any_space] * 12,
        out_specs=(vmem,) * 3,
        scratch_shapes=[
            pltpu.VMEM((4, LEVELS, ROWS + 16, COLS), f32),
            pltpu.VMEM((4, LEVELS, ROWS + 16, COLS), f32),
            pltpu.VMEM((4, LEVELS, ROWS, COLS), f32),
            pltpu.VMEM((LEVELS, ROWS, COLS), f32),
            pltpu.VMEM((LEVELS, ROWS, COLS), f32),
            pltpu.VMEM((2, LEVELS, ROWS, COLS), f32),
            pltpu.VMEM((LEVELS, ROWS, COLS), f32),
            pltpu.VMEM((4, LEVELS, ROWS, COLS), f32),
            pltpu.VMEM((2 * COLS, 2 * COLS), jnp.bfloat16),
            pltpu.VMEM((2 * COLS, 2 * COLS), jnp.bfloat16),
            pltpu.VMEM((2, n_z - 1, per, ROWS // 2, COLS), f32),
            pltpu.VMEM((2, 2, 2, 16, 4, COLS), f32),
            pltpu.VMEM((2, 2, 2, 16, 4, COLS), f32),
            pltpu.VMEM((2, 2, 2, ROWS // 2, COLS), f32),
            pltpu.VMEM((2, 2, 2, ROWS // 2, COLS), f32),
            pltpu.VMEM((2, ROWS, COLS), f32),
            pltpu.VMEM((2, 32, 16, COLS), f32),
            pltpu.VMEM((2, ROWS, COLS), f32),
            pltpu.VMEM((7, ROWS, COLS), f32),
            pltpu.VMEM((2,) + tile, f32),
            pltpu.VMEM((n_y,) + tile, f32),
            pltpu.VMEM((n_x,) + tile, f32),
            pltpu.VMEM((n_z,) + tile, f32),
            pltpu.SMEM(args[4].shape, jnp.int32),
            pltpu.SMEM(args[5].shape, jnp.int32),
            pltpu.SMEM((1,), jnp.int32),
            pltpu.SMEM((1,), jnp.int32),
            pltpu.SMEM(args[8].shape, f32),
            pltpu.VMEM(args[9].shape, jnp.int32),
            pltpu.VMEM(args[10].shape, jnp.int32),
            pltpu.VMEM(args[11].shape, f32),
            dma((5,)),
            dma((8,)),
            dma((2, 2, 2, 2)),
            dma((2, 2, 2, 2)),
            dma((2, 2)),
            dma((2, 2, n_z - 1)),
            dma((2, 2, n_z - 1)),
            dma((2, 2, n_z)),
            dma((2,)),
            dma((2, n_y - 1)),
            dma((2, n_x - 1)),
            dma((2, n_z - 1)),
            pltpu.SemaphoreType.REGULAR((3,)),
        ],
        compiler_params=pltpu.CompilerParams(
            collective_id=0, has_side_effects=True, vmem_limit_bytes=32 * 1024 * 1024
        ),
    )(*[arg if arg.size == 1 else pltpu.with_memory_space_constraint(arg, pltpu.HBM) for arg in args])
    sums_shape = jax.ShapeDtypeStruct((LEVELS, ROWS, COLS), f32)
    fields, grad, hess, curv = pl.pallas_call(
        deliver,
        out_shape=(jax.ShapeDtypeStruct(fields.shape, f32), sums_shape, sums_shape, jax.ShapeDtypeStruct((1, 1), f32)),
        in_specs=[any_space] * 3,
        out_specs=(hbm,) * 4,
        scratch_shapes=[dma((4,))],
    )(*[pltpu.with_memory_space_constraint(value, pltpu.VMEM) for value in (fields, sums, curv)])
    return fields, grad, hess, curv[0, 0]


def solution(mesh):
    sizes = (mesh.shape["shot"], mesh.shape["gx"], mesh.shape["gy"])
    placed = (
        P("shot", None, None, "gx", "gy"),
        P("shot", None, None, "gx", "gy"),
        P(None, "gx", "gy"),
        P(None, "gx", "gy"),
        P(),
        P(),
        P("shot"),
        P("shot"),
        P("shot", None),
        P("shot", None),
        P("shot", None),
        P("shot", None, None),
    )
    return jax.shard_map(
        functools.partial(local, sizes),
        mesh=mesh,
        in_specs=placed,
        out_specs=(
            P("shot", None, None, "gx", "gy"),
            P(None, "gx", "gy"),
            P(None, "gx", "gy"),
            P(),
        ),
        check_vma=False,
    )
```
